256 devices in a mesh: dp: 4 (over z_lo, core), seq: 64 (over z_hi, x, y).
Axes of the slice: x: 4, y: 4, z: 8 (z_hi: 4, z_lo: 2; z = z_hi * 2 + z_lo), core: 2. Of those that a mesh axis runs over, the one named last changes fastest.
Arguments:
- tokens: bfloat16 [4, 65536, 768], P('dp', 'seq'), may hold values from -16 to 16
- first_factor: bfloat16 [256, 256, 256], P('seq'), may hold values from -0.375 to 0.375
- second_factor: bfloat16 [256, 256, 256], P('seq'), may hold values from -0.375 to 0.375
- value_weight: bfloat16 [768, 768], replicated, may hold values from -0.21875 to 0.21875
- gate_weight: bfloat16 [768, 768], replicated, may hold values from -0.21875 to 0.21875
- out_weight: bfloat16 [768, 768], replicated, may hold values from -0.21875 to 0.21875
- cotangent: bfloat16 [4, 65536, 768], P('dp', 'seq'), may hold values from -16 to 16
Outputs:
- result: bfloat16 [4, 65536, 768], P('dp', 'seq')
- grad_tokens: bfloat16 [4, 65536, 768], P('dp', 'seq')
- grad_first: float32 [256, 256, 256], P('seq')
- grad_second: float32 [256, 256, 256], P('seq')
- grad_value: float32 [768, 768], P('seq')
- grad_gate: float32 [768, 768], P('seq')
- grad_out: float32 [768, 768], P('seq')
The draws below stay inside these ranges and needn't reach their ends.
All inputs are finite; a program needn't handle non-finite values.
Results may differ from the reference program's by a relative error of at most 0.014.
Values may be sent and summed in bfloat16 or wider, within the bound.
A program may use at most 128 MiB of HBM per device.

```python
import jax
import jax.numpy as jnp

A = 256
B = 256
D = 768
L = 65536
SEQS = 4
N_DP = 4


def with_spikes(drawn, rng, source, target, blocks, factor):
    owner, partner = [(jnp.arange(drawn.shape[axis_at]) // (drawn.shape[axis_at] // blocks)).reshape([-1 if axis == axis_at else 1 for axis in range(drawn.ndim)]) for axis_at in (source, target)]
    chosen = jax.random.permutation(rng, blocks)[partner]
    strong = (owner == chosen) | (owner == (partner + blocks // 2) % blocks)
    return jnp.where(strong, factor * drawn, drawn)


def steps_of(rng, shape, split, least, top_value):
    loudness, own = 1.0, jax.random.fold_in(rng, 6)
    for dim, blocks in split:
        steps = jnp.exp(jax.random.uniform(jax.random.fold_in(own, dim), (blocks,), jnp.float32, least / len(split), top_value / len(split)))
        loudness = loudness * jnp.repeat(steps, shape[dim] // blocks).reshape([-1 if axis == dim else 1 for axis in range(len(shape))])
    return loudness


def normal_values(key, dims, spread, reach, cuts=(), held_as=jnp.bfloat16):
    level = steps_of(key, dims, cuts, -0.22, 0.18) if cuts else 1.0
    values = jax.random.normal(key, dims, jnp.float32) * spread * level
    return jnp.minimum(jnp.maximum(values, -reach), reach).astype(held_as)


def heavy_noise(own_key, shape, scale, reach, cuts, heavy, held_as=jnp.bfloat16):
    values = scale * jax.random.normal(own_key, shape, jnp.float32)
    if cuts:
        values = values * steps_of(own_key, shape, cuts, -0.22, 0.18)
    return jnp.clip(with_spikes(values, jax.random.fold_in(own_key, 3), *heavy), -reach, reach).astype(held_as)


def setup_inputs(seed: int = 0) -> dict:
    key_of = jax.random.split(jax.random.key(seed), 8)
    return {
        "tokens": heavy_noise(key_of[0], (SEQS, L, D), 1.0, 16.0, ((0, 4), (1, 64)), (1, 2, 64, 4.0)),
        "first_factor": normal_values(key_of[1], (A, B, B), B ** -0.5, 0.375, ((0, 64),)),
        "second_factor": normal_values(key_of[2], (B, A, A), A ** -0.5, 0.375, ((0, 64),)),
        "value_weight": normal_values(key_of[3], (D, D), D ** -0.5, 0.21875),
        "gate_weight": normal_values(key_of[4], (D, D), D ** -0.5, 0.21875),
        "out_weight": normal_values(key_of[5], (D, D), D ** -0.5, 0.21875),
        "cotangent": heavy_noise(key_of[6], (SEQS, L, D), 1.0, 16.0, ((0, 4), (1, 64)), (1, 2, 64, 4.0)),
    }


def one_sequence(rows_in, cot_rows, first_factor, second_factor, value_weight, gate_weight, out_weight):
    value = jnp.dot(rows_in, value_weight, preferred_element_type=jnp.float32)
    gated = jnp.dot(rows_in, gate_weight, preferred_element_type=jnp.float32)
    sigma = jax.nn.sigmoid(gated)
    mixed_in = (value * sigma).astype(jnp.bfloat16)
    cube_in = mixed_in.reshape(A, B, D)
    first_pass = jnp.einsum('apb,abd->apd', first_factor.astype(jnp.float32), cube_in.astype(jnp.float32)).astype(jnp.bfloat16)
    second_pass = jnp.einsum('pqa,apd->pqd', second_factor.astype(jnp.float32), first_pass.astype(jnp.float32)).astype(jnp.bfloat16)
    flat_second = second_pass.reshape(L, D)
    result = jnp.dot(flat_second, out_weight, preferred_element_type=jnp.float32).astype(jnp.bfloat16)
    back_second = jnp.dot(cot_rows, out_weight.T, preferred_element_type=jnp.float32).astype(jnp.bfloat16)
    out_term = jnp.dot(flat_second.T, cot_rows, preferred_element_type=jnp.float32)
    back_cube = back_second.reshape(B, A, D).astype(jnp.float32)
    back_first = jnp.einsum('pqa,pqd->apd', second_factor.astype(jnp.float32), back_cube).astype(jnp.bfloat16)
    second_term = jnp.einsum('pqd,apd->pqa', back_cube, first_pass.astype(jnp.float32))
    back_mixed = jnp.einsum('apb,apd->abd', first_factor.astype(jnp.float32), back_first.astype(jnp.float32)).reshape(L, D)
    first_term = jnp.einsum('apd,abd->apb', back_first.astype(jnp.float32), cube_in.astype(jnp.float32))
    dvalue = (back_mixed * sigma).astype(jnp.bfloat16)
    dgate = (back_mixed * value * sigma * (1.0 - sigma)).astype(jnp.bfloat16)
    grad_rows = (jnp.dot(dvalue, value_weight.T, preferred_element_type=jnp.float32)
                 + jnp.dot(dgate, gate_weight.T, preferred_element_type=jnp.float32)).astype(jnp.bfloat16)
    value_term = jnp.dot(rows_in.T, dvalue, preferred_element_type=jnp.float32)
    gate_term = jnp.dot(rows_in.T, dgate, preferred_element_type=jnp.float32)
    return result, grad_rows, first_term, second_term, value_term, gate_term, out_term


def reference(tokens, first_factor, second_factor, value_weight, gate_weight, out_weight, cotangent):
    results = []
    grads_in = []
    first_sum = jnp.zeros((A, B, B), jnp.float32)
    second_sum = jnp.zeros((B, A, A), jnp.float32)
    value_sum = jnp.zeros((D, D), jnp.float32)
    gate_sum = jnp.zeros((D, D), jnp.float32)
    out_sum = jnp.zeros((D, D), jnp.float32)
    for group in range(N_DP):
        parts = one_sequence(tokens[group], cotangent[group], first_factor, second_factor, value_weight, gate_weight, out_weight)
        results.append(parts[0])
        grads_in.append(parts[1])
        first_sum = first_sum + parts[2]
        second_sum = second_sum + parts[3]
        value_sum = value_sum + parts[4]
        gate_sum = gate_sum + parts[5]
        out_sum = out_sum + parts[6]
    return jnp.stack(results), jnp.stack(grads_in), first_sum, second_sum, value_sum, gate_sum, out_sum
```

```python
import jax
import jax.numpy as jnp
from jax import lax
from jax.experimental import pallas as pl
from jax.experimental.pallas import tpu as pltpu
from jax.sharding import PartitionSpec as P

MESH = pl.DeviceIdType.MESH
BF16 = jnp.bfloat16
F32 = jnp.float32


def contract_rows(left, right):
    return lax.dot_general(left, right, (((0,), (0,)), ((), ())), preferred_element_type=F32)


def contract_cols(left, right):
    return lax.dot_general(left, right, (((1,), (1,)), ((), ())), preferred_element_type=F32)


def exchange_kernel(a_ref, b_ref, a_out, b_out, send_sem, recv_sem):
    dp, seq = lax.axis_index("dp"), lax.axis_index("seq")
    barrier = pltpu.get_barrier_semaphore()

    def peer(step):
        return lax.rem(seq + step, 64)

    def greet(step, carry):
        pl.semaphore_signal(barrier, inc=1, device_id=(dp, peer(step)), device_id_type=MESH)
        return carry

    lax.fori_loop(1, 64, greet, 0)
    pl.semaphore_wait(barrier, 63)
    for k, (src, dst) in enumerate(((a_ref, a_out), (b_ref, b_out))):

        def send(step, carry, src=src, dst=dst, k=k):
            pltpu.make_async_remote_copy(
                src_ref=src.at[peer(step)],
                dst_ref=dst.at[seq],
                send_sem=send_sem.at[k],
                recv_sem=recv_sem.at[k],
                device_id=(dp, peer(step)),
                device_id_type=MESH,
            ).start()
            return carry

        lax.fori_loop(1, 64, send, 0)
        dst[seq] = src[seq]
    for k, (src, dst) in enumerate(((a_ref, a_out), (b_ref, b_out))):
        whole = pltpu.make_async_remote_copy(
            src_ref=src.at[pl.ds(0, 63)],
            dst_ref=dst.at[pl.ds(0, 63)],
            send_sem=send_sem.at[k],
            recv_sem=recv_sem.at[k],
            device_id=(dp, peer(1)),
            device_id_type=MESH,
        )
        whole.wait_send()
        whole.wait_recv()


def exchange(a, b):
    shape = jax.ShapeDtypeStruct((64, 16, 768), BF16)
    vmem = pl.BlockSpec(memory_space=pltpu.VMEM)
    return pl.pallas_call(
        exchange_kernel,
        out_shape=(shape, shape),
        in_specs=[vmem] * 2,
        out_specs=(vmem, vmem),
        scratch_shapes=[pltpu.SemaphoreType.DMA((2,)), pltpu.SemaphoreType.DMA((2,))],
        compiler_params=pltpu.CompilerParams(
            collective_id=0, has_side_effects=True, vmem_limit_bytes=32 * 2**20
        ),
        name="exchange",
    )(a, b)


def reduce_kernel(
    w_ref, f_ref, w_out, f_out, w_r0, u, r1, wsum, r2, f_r0, f_s, f_r1, f_t, send_sem, recv_sem
):
    dp, seq = lax.axis_index("dp"), lax.axis_index("seq")
    zl, core = dp // 2, lax.rem(dp, 2)
    zh, xy = seq // 16, lax.rem(seq, 16)
    z = zh * 2 + zl
    other = 1 - core
    barrier = pltpu.get_barrier_semaphore()

    def copy(src, dst, k, device):
        return pltpu.make_async_remote_copy(
            src_ref=src,
            dst_ref=dst,
            send_sem=send_sem.at[k],
            recv_sem=recv_sem.at[k],
            device_id=device,
            device_id_type=MESH,
        )

    def plane(step):
        to = lax.rem(xy + step, 16)
        return to, (dp, zh * 16 + to)

    def column(step):
        to = lax.rem(z * 2 + core + step, 16)
        to_z, to_core = to // 2, lax.rem(to, 2)
        return to_z // 2, (lax.rem(to_z, 2) * 2 + to_core, (to_z // 2) * 16 + xy)

    def greet(step, carry):
        pl.semaphore_signal(barrier, inc=1, device_id=plane(step)[1], device_id_type=MESH)
        pl.semaphore_signal(barrier, inc=1, device_id=column(step)[1], device_id_type=MESH)
        return carry

    lax.fori_loop(1, 16, greet, 0)
    pl.semaphore_wait(barrier, 30)
    partner = (zl * 2 + other, seq)
    neighbour = ((1 - zl) * 2 + core, seq)

    s0 = copy(w_ref.at[other], w_r0, 0, partner)
    s0.start()
    g0 = copy(f_ref.at[other], f_r0, 1, partner)
    g0.start()
    s0.wait()

    def add_pair(i, carry):
        u[i] = (w_ref[core, i].astype(F32) + w_r0[i].astype(F32)).astype(BF16)
        return carry

    lax.fori_loop(0, 16, add_pair, 0)

    def send_plane(step, carry):
        to, device = plane(step)
        copy(u.at[to], r1.at[xy], 2, device).start()
        return carry

    lax.fori_loop(1, 16, send_plane, 0)
    r1[xy] = u[xy]
    g0.wait()

    def add_factor(i, carry):
        rows = pl.ds(pl.multiple_of(i * 128, 128), 128)
        f_s[rows, :] = (f_ref[core, rows, :].astype(F32) + f_r0[rows, :].astype(F32)).astype(BF16)
        return carry

    lax.fori_loop(0, 8, add_factor, 0)
    g1 = copy(f_s, f_r1, 3, neighbour)
    g1.start()
    copy(u.at[pl.ds(0, 15)], r1.at[pl.ds(0, 15)], 2, plane(1)[1]).wait()

    def add_plane(q, carry):
        total = r1[0, q].astype(F32)
        for i in range(1, 16):
            total = total + r1[i, q].astype(F32)
        wsum[q] = total.astype(BF16)
        return carry

    lax.fori_loop(0, 4, add_plane, 0)

    def send_column(step, carry):
        to, device = column(step)
        copy(wsum.at[to], r2.at[core * 8 + z], 4, device).start()
        return carry

    lax.fori_loop(1, 16, send_column, 0)
    r2[core * 8 + z] = wsum[zh]
    g1.wait()

    def add_neighbour(i, carry):
        rows = pl.ds(pl.multiple_of(i * 128, 128), 128)
        f_t[core, rows, :] = (f_s[rows, :].astype(F32) + f_r1[rows, :].astype(F32)).astype(BF16)
        return carry

    lax.fori_loop(0, 8, add_neighbour, 0)
    g2 = copy(f_t.at[core], f_t.at[core], 5, partner)
    g2.start()
    copy(r2.at[pl.ds(0, 15)], r2.at[pl.ds(0, 15)], 4, partner).wait()
    for half in range(2):
        total = r2[half * 8].astype(F32)
        for i in range(1, 8):
            total = total + r2[half * 8 + i].astype(F32)
        w_out[:, half * 384 : (half + 1) * 384] = total
    g2.wait()
    f_out[...] = f_t[...].astype(F32)


def reduce_all(w, f):
    vmem = pl.BlockSpec(memory_space=pltpu.VMEM)
    return pl.pallas_call(
        reduce_kernel,
        out_shape=(
            jax.ShapeDtypeStruct((48, 768), F32),
            jax.ShapeDtypeStruct((2, 1024, 256), F32),
        ),
        in_specs=[vmem] * 2,
        out_specs=(vmem, vmem),
        scratch_shapes=[
            pltpu.VMEM((16, 4, 48, 384), BF16),
            pltpu.VMEM((16, 4, 48, 384), BF16),
            pltpu.VMEM((16, 4, 48, 384), BF16),
            pltpu.VMEM((4, 48, 384), BF16),
            pltpu.VMEM((16, 48, 384), BF16),
            pltpu.VMEM((1024, 256), BF16),
            pltpu.VMEM((1024, 256), BF16),
            pltpu.VMEM((1024, 256), BF16),
            pltpu.VMEM((2, 1024, 256), BF16),
            pltpu.SemaphoreType.DMA((6,)),
            pltpu.SemaphoreType.DMA((6,)),
        ],
        compiler_params=pltpu.CompilerParams(
            collective_id=1, has_side_effects=True, vmem_limit_bytes=40 * 2**20
        ),
        name="reduce",
    )(w, f)


def shards(tokens, first_factor, second_factor, value_weight, gate_weight, out_weight, cotangent):
    rows_in = tokens[0]
    cot_rows = cotangent[0]
    back_second = contract_cols(cot_rows, out_weight).astype(BF16).reshape(4, 256, 768)
    back_first = jnp.einsum(
        "pqa,pqd->apd", second_factor, back_second, preferred_element_type=F32
    ).astype(BF16)
    value = jnp.dot(rows_in, value_weight, preferred_element_type=F32)
    gated = jnp.dot(rows_in, gate_weight, preferred_element_type=F32)
    sigma = jax.nn.sigmoid(gated)
    cube_in = (value * sigma).astype(BF16).reshape(4, 256, 768)
    first_pass = jnp.einsum(
        "apb,abd->pad", first_factor, cube_in, preferred_element_type=F32
    ).astype(BF16)
    back_got, first_got = exchange(
        back_first.reshape(64, 16, 768), first_pass.reshape(64, 16, 768)
    )
    back_cube = back_got.reshape(64, 4, 4, 768)
    first_cube = first_got.reshape(64, 4, 4, 768)
    piece = back_cube.transpose(1, 0, 2, 3).reshape(4, 256, 768)
    back_mixed = jnp.einsum("apb,apd->abd", first_factor, piece, preferred_element_type=F32)
    first_term = jnp.einsum("apd,abd->apb", piece, cube_in, preferred_element_type=F32)
    back_flat = back_mixed.reshape(1024, 768)
    dvalue = (back_flat * sigma).astype(BF16)
    dgate = (back_flat * value * sigma * (1.0 - sigma)).astype(BF16)
    grad_rows = (contract_cols(dvalue, value_weight) + contract_cols(dgate, gate_weight)).astype(
        BF16
    )
    value_term = contract_rows(rows_in, dvalue)
    gate_term = contract_rows(rows_in, dgate)
    received = first_cube.transpose(1, 0, 2, 3).reshape(4, 256, 768)
    second_pass = jnp.einsum(
        "pqa,pad->pqd", second_factor, received, preferred_element_type=F32
    ).astype(BF16)
    flat_second = second_pass.reshape(1024, 768)
    result = jnp.dot(flat_second, out_weight, preferred_element_type=F32).astype(BF16)
    out_term = contract_rows(flat_second, cot_rows)
    second_term = jnp.einsum("pqd,pad->pqa", back_second, received, preferred_element_type=F32)
    w = jnp.stack([value_term, gate_term, out_term]).astype(BF16)
    w = jnp.pad(w.reshape(3, 4, 16, 12, 2, 384), ((0, 0), (0, 0), (0, 0), (0, 4), (0, 0), (0, 0)))
    w = w.transpose(4, 2, 1, 0, 3, 5).reshape(2, 16, 4, 48, 384)
    f = jnp.stack([first_term, second_term]).astype(BF16).reshape(2, 2, 512, 256)
    f = f.transpose(1, 0, 2, 3).reshape(2, 1024, 256)
    w_sum, f_sum = reduce_all(w, f)
    w_sum = w_sum.reshape(3, 16, 768)[:, :12]
    f_sum = f_sum.reshape(2, 2, 512, 256).transpose(1, 0, 2, 3).reshape(2, 4, 256, 256)
    return (
        result[None],
        grad_rows[None],
        f_sum[0],
        f_sum[1],
        w_sum[0],
        w_sum[1],
        w_sum[2],
    )


def solution(mesh):
    return jax.shard_map(
        shards,
        mesh=mesh,
        in_specs=(
            P("dp", "seq", None),
            P("seq", None, None),
            P("seq", None, None),
            P(),
            P(),
            P(),
            P("dp", "seq", None),
        ),
        out_specs=(
            P("dp", "seq", None),
            P("dp", "seq", None),
            P("seq", None, None),
            P("seq", None, None),
            P("seq", None),
            P("seq", None),
            P("seq", None),
        ),
        check_vma=False,
    )
```

```python
import functools

import jax
import jax.numpy as jnp
from jax import lax
from jax.experimental import pallas as pl
from jax.experimental.pallas import tpu as pltpu
from jax.sharding import PartitionSpec as P

MESH = pl.DeviceIdType.MESH
BF16 = jnp.bfloat16
F32 = jnp.float32
NZ, NX = 4, 16


def dot(left, right):
    return jnp.dot(left, right, preferred_element_type=F32)


def dot_cols(left, right):
    return lax.dot_general(left, right, (((1,), (1,)), ((), ())), preferred_element_type=F32)


def each(count, body):
    def step(i, carry):
        body(i)
        return carry

    lax.fori_loop(0, count, step, 0)


def mega(nz, nx, *refs):
    ns = nz * nx
    rows = 4 * ns
    width = 12 * ns
    half = width // 2
    lanes = half // 3
    (tok_h, ff_h, sf_h, vw_h, gw_h, ow_h, cot_h), refs = refs[:7], refs[7:]
    (res_h, grad_h, first_out, second_out, w_out), refs = refs[:5], refs[5:]
    (tok, ff, sf, vw, gw, ow, cot, tok_t, ff_t, sf_t), refs = refs[:10], refs[10:]
    (bs, bsend, brecv, fsend, frecv, val, sig, mix), refs = refs[:8], refs[8:]
    (tmp, got, dval, dgate, sec, sec_t, res, grad), refs = refs[:8], refs[8:]
    (first, second, term, wide), refs = refs[:4], refs[4:]
    jobs = [refs[7 * n : 7 * n + 7] for n in range(4)]
    refs = refs[28:]
    facs = [refs[5 * n : 5 * n + 5] for n in range(2)]
    refs = refs[10:]
    load_sem, store_sem, a2a_send, a2a_recv, job_send, job_recv, fac_send, fac_recv = refs
    a2a, job, fac = (a2a_send, a2a_recv), (job_send, job_recv), (fac_send, fac_recv)

    dp, seq = lax.axis_index("dp"), lax.axis_index("seq")
    zl, core = dp // 2, lax.rem(dp, 2)
    zh, xy = seq // nx, lax.rem(seq, nx)
    z = zh * 2 + zl
    other = 1 - core
    partner = (zl * 2 + other, seq)
    neighbour = ((1 - zl) * 2 + core, seq)

    loads = [
        pltpu.make_async_copy(src, dst, load_sem.at[i])
        for i, (src, dst) in enumerate(
            ((cot_h, cot), (ow_h, ow), (sf_h, sf), (tok_h, tok), (vw_h, vw), (gw_h, gw), (ff_h, ff))
        )
    ]
    for load in loads:
        load.start()

    barrier = pltpu.get_barrier_semaphore()

    def peer(step):
        return lax.rem(seq + step, ns)

    def greet(i):
        pl.semaphore_signal(barrier, inc=1, device_id=(dp, peer(i + 1)), device_id_type=MESH)

    def greet_column(i):
        device = ((1 - zl) * 2 + core, i * nx + xy)
        pl.semaphore_signal(barrier, inc=1, device_id=device, device_id_type=MESH)

    each(ns - 1, greet)
    each(nz, greet_column)
    pl.semaphore_signal(barrier, inc=1, device_id=partner, device_id_type=MESH)

    def remote(src, dst, sems, k, device):
        return pltpu.make_async_remote_copy(
            src_ref=src,
            dst_ref=dst,
            send_sem=sems[0].at[k],
            recv_sem=sems[1].at[k],
            device_id=device,
            device_id_type=MESH,
        )

    def send_all(src, dst, k):
        def send(i):
            to = peer(i + 1)
            remote(src.at[to], dst.at[seq], a2a, k, (dp, to)).start()

        each(ns - 1, send)
        dst[seq] = src[seq]

    def all_of(src, dst, k):
        return remote(src.at[pl.ds(0, ns - 1)], dst.at[pl.ds(0, ns - 1)], a2a, k, (dp, peer(1)))

    def to_messages(dst):
        tiles = min(8, rows // 8)
        mask = lax.broadcasted_iota(jnp.int32, (tiles, 8, half), 1) < 4

        def block(i):
            at = pl.ds(pl.multiple_of(i * tiles * 8, 8), tiles * 8)
            r = [tmp[k, at, :].reshape(tiles, 8, half) for k in range(4)]
            turned = [pltpu.roll(x, 4, 1) for x in r]
            low = [jnp.where(mask, r[k], turned[k + 1]) for k in (0, 2)]
            high = [jnp.where(mask, turned[k], r[k + 1]) for k in (0, 2)]
            low = jnp.concatenate(low, axis=1).astype(BF16)
            high = jnp.concatenate(high, axis=1).astype(BF16)
            for t in range(tiles):
                dst[(i * tiles + t) * 2] = low[t]
                dst[(i * tiles + t) * 2 + 1] = high[t]

        each(rows // (tiles * 8), block)

    def from_messages(src):
        for j in range(3):
            cols = slice(j * lanes, (j + 1) * lanes)

            def widen(i, j=j, cols=cols):
                at = pl.ds(pl.multiple_of(i * 64, 64), 64)
                part = src[pl.ds(i * 4, 4), :, cols]
                term[j, at, :] = part.reshape(64, lanes).astype(F32)

            each(4 * rows // 64, widen)
            for k in range(4):
                got[k, :, cols] = term[j, pl.ds(k, rows, stride=4), :].astype(BF16)

    def zone(n):
        count = nz if n < 2 else nz // 2
        base = 0 if n < 2 else (n - 2) * count
        member = (zh >= base) & (zh < base + count)
        return count, base, member

    def put_rows(n, which):
        own = jobs[n][0]

        def two(m):
            x = wide[pl.ds(pl.multiple_of(24 * m, 8), 32), :]
            for k in range(2):
                s = 2 * m + k
                block = x[12 * k : 12 * k + 16].astype(BF16)
                own[which, lax.rem(s, nx), s // nx] = block

        each(zone(n)[0] * nx // 2, two)

    def pair_copy(n):
        return remote(jobs[n][0].at[other], jobs[n][1], job, 4 * n, partner)

    def pair_add(n):
        own, pair, u, plane = jobs[n][:4]
        pair_copy(n).wait()

        def add(i):
            u[i] = (own[core, i].astype(F32) + pair[i].astype(F32)).astype(BF16)

        each(nx, add)

        def send(i):
            to = lax.rem(xy + i + 1, nx)
            remote(u.at[to], plane.at[xy], job, 4 * n + 1, (dp, zh * nx + to)).start()

        each(nx - 1, send)
        plane[xy] = u[xy]

    def plane_add(n):
        u, plane, total, col = jobs[n][2:6]
        count, base, member = zone(n)
        remote(
            u.at[pl.ds(0, nx - 1)], plane.at[pl.ds(0, nx - 1)], job, 4 * n + 1, partner
        ).wait()

        def add(q):
            x = plane[0, q].astype(F32)
            for i in range(1, nx):
                x = x + plane[i, q].astype(F32)
            total[q] = x.astype(BF16)

        each(count, add)

        def send(i):
            to_zh, to_zl = base + i // 2, lax.rem(i, 2)

            @pl.when(to_zh * 2 + to_zl != z)
            def _():
                device = (to_zl * 2 + core, to_zh * nx + xy)
                remote(total.at[i // 2], col.at[z], job, 4 * n + 2, device).start()

        each(2 * count, send)

        @pl.when(member)
        def _():
            col[z] = total[zh - base]

    def column_add(n):
        col, fin = jobs[n][5:]
        count, _, member = zone(n)

        def part(size):
            return remote(
                col.at[pl.ds(0, size)], col.at[pl.ds(0, size)], job, 4 * n + 2, partner
            )

        @pl.when(member)
        def _():
            part(2 * nz - 1).wait_recv()
            x = col[0].astype(F32)
            for i in range(1, 2 * nz):
                x = x + col[i].astype(F32)
            fin[core] = x.astype(BF16)
            remote(fin.at[core], fin.at[core], job, 4 * n + 3, partner).start()
            part(2 * count - 1).wait_send()

        @pl.when(jnp.logical_not(member))
        def _():
            part(2 * count).wait_send()

    def finish(n):
        fin = jobs[n][6]

        @pl.when(zone(n)[2])
        def _():
            remote(fin.at[core], fin.at[core], job, 4 * n + 3, partner).wait()
            at = [
                ((0, slice(0, half)), (1, slice(0, half))),
                ((0, slice(half, width)), (1, slice(half, width))),
                ((2, slice(0, half)), (2, slice(half, width))),
                ((2, slice(0, half)), (2, slice(half, width))),
            ][n]
            for k in range(2):
                w_out[at[k][0], :, at[k][1]] = fin[k].astype(F32)

    def factor_start(n, source):
        own, pair = facs[n][:2]
        for k in range(4):
            own[k // 2, k % 2] = source[k].astype(BF16)
        remote(own.at[other], pair, fac, 3 * n, partner).start()

    def factor_pair(n):
        own, pair, u, near = facs[n][:4]
        remote(own.at[other], pair, fac, 3 * n, partner).wait()

        def add(k):
            u[k] = (own[core, k].astype(F32) + pair[k].astype(F32)).astype(BF16)

        each(2, add)
        remote(u, near, fac, 3 * n + 1, neighbour).start()

    def factor_near(n):
        _, _, u, near, fin = facs[n]
        remote(u, near, fac, 3 * n + 1, neighbour).wait()

        def add(k):
            fin[core, k] = (u[k].astype(F32) + near[k].astype(F32)).astype(BF16)

        each(2, add)
        remote(fin.at[core], fin.at[core], fac, 3 * n + 2, partner).start()

    def factor_end(n, store):
        fin = facs[n][4]
        remote(fin.at[core], fin.at[core], fac, 3 * n + 2, partner).wait()
        store.start()

    stores = [
        pltpu.make_async_copy(src, dst, store_sem.at[i])
        for i, (src, dst) in enumerate(
            (
                (res, res_h),
                (grad, grad_h),
                (facs[0][4], first_out),
                (facs[1][4], second_out),
            )
        )
    ]

    wide[width:, :] = jnp.zeros((8, half), F32)

    for load in loads[:3]:
        load.wait()
    for k in range(4):
        sf_t[k] = sf[k].T
    for c in range(2):

        def back(p, c=c):
            part = dot_cols(cot[p], ow[c * half : (c + 1) * half, :]).astype(BF16)
            bs[c, p] = part
            tmp[p] = dot(sf_t[p], part)

        each(4, back)
        to_messages(bsend.at[c])
        if c == 0:
            pl.semaphore_wait(barrier, ns + nz)
        send_all(bsend.at[c], brecv.at[c], c)

    for load in loads[3:]:
        load.wait()
    for c in range(2):
        cols = slice(c * half, (c + 1) * half)

        def forward(a, c=c, cols=cols):
            v = dot(tok[a], vw[:, cols])
            s = jax.nn.sigmoid(dot(tok[a], gw[:, cols]))
            m = (v * s).astype(BF16)
            val[c, a] = v
            sig[c, a] = s
            mix[c, a] = m
            tmp[a] = dot(ff[a], m)

        each(4, forward)
        to_messages(fsend.at[c])
    for k in range(4):
        ff_t[k] = ff[k].T
        tok_t[:, k * rows : (k + 1) * rows] = tok[k].T

    for c in range(2):
        all_of(bsend.at[c], brecv.at[c], c).wait_send()
        send_all(fsend.at[c], frecv.at[c], 2 + c)
        all_of(bsend.at[c], brecv.at[c], c).wait_recv()
        from_messages(brecv.at[c])

        def inner(a, c=c):
            g = got[a]
            part = dot(ff_t[a], g)
            s = sig[c, a]
            ps = part * s
            dval[c, a] = ps.astype(BF16)
            dgate[c, a] = (ps * val[c, a] * (1.0 - s)).astype(BF16)
            more = dot_cols(g, mix[c, a])
            if c == 0:
                first[a] = more
            else:
                first[a] = first[a] + more

        each(4, inner)
        for which, source in enumerate((dval, dgate)):

            def terms(m, c=c, source=source):
                at = pl.ds(pl.multiple_of(m * rows, 8), rows)
                wide[at, :] = dot(tok_t[at, :], source[c].reshape(4 * rows, half))

            each(3, terms)
            put_rows(c, which)
        pair_copy(c).start()
    factor_start(0, first)
    pair_add(0)
    pair_add(1)
    factor_pair(0)

    def grads(a):
        x = dot_cols(dval[0, a], vw[:, :half]) + dot_cols(dval[1, a], vw[:, half:])
        y = dot_cols(dgate[0, a], gw[:, :half]) + dot_cols(dgate[1, a], gw[:, half:])
        grad[a] = (x + y).astype(BF16)

    each(4, grads)
    stores[1].start()

    def second_half(c):
        all_of(fsend.at[c], frecv.at[c], 2 + c).wait()
        from_messages(frecv.at[c])

        def inner(p):
            sec[c, p] = dot(sf[p], got[p]).astype(BF16)

        each(4, inner)
        for k in range(4):
            sec_t[:, k * rows : (k + 1) * rows] = sec[c, k].T
        for which in range(2):
            cols = slice(which * half, (which + 1) * half)
            wide[:half, :] = dot(sec_t[...], cot[:, :, cols].reshape(4 * rows, half))
            put_rows(2 + c, which)
        pair_copy(2 + c).start()

        def outer(p):
            more = dot_cols(bs[c, p], got[p])
            if c == 0:
                second[p] = more
            else:
                second[p] = second[p] + more

        each(4, outer)

    second_half(0)
    plane_add(0)
    plane_add(1)
    factor_near(0)
    pair_add(2)
    second_half(1)
    factor_start(1, second)
    pair_add(3)
    factor_pair(1)
    column_add(0)
    column_add(1)
    plane_add(2)

    def results(p):
        x = dot(sec[0, p], ow[:half, :]) + dot(sec[1, p], ow[half:, :])
        res[p] = x.astype(BF16)

    each(4, results)
    stores[0].start()
    factor_end(0, stores[2])
    plane_add(3)
    factor_near(1)
    column_add(2)
    column_add(3)
    factor_end(1, stores[3])
    for n in range(4):
        finish(n)
    for store in stores:
        store.wait()


def mega_call(nz, nx, *args):
    ns = nz * nx
    rows = 4 * ns
    width = 12 * ns
    half = width // 2
    vmem, sem = pltpu.VMEM, pltpu.SemaphoreType.DMA
    scratch = [
        vmem((4, rows, width), BF16),
        vmem((4, rows, rows), BF16),
        vmem((4, rows, rows), BF16),
        vmem((width, width), BF16),
        vmem((width, width), BF16),
        vmem((width, width), BF16),
        vmem((4, rows, width), BF16),
        vmem((width, 4 * rows), BF16),
        vmem((4, rows, rows), BF16),
        vmem((4, rows, rows), BF16),
        vmem((2, 4, rows, half), BF16),
        vmem((2, ns, 16, half), BF16),
        vmem((2, ns, 16, half), BF16),
        vmem((2, ns, 16, half), BF16),
        vmem((2, ns, 16, half), BF16),
        vmem((2, 4, rows, half), F32),
        vmem((2, 4, rows, half), F32),
        vmem((2, 4, rows, half), BF16),
        vmem((4, rows, half), F32),
        vmem((4, rows, half), BF16),
        vmem((2, 4, rows, half), BF16),
        vmem((2, 4, rows, half), BF16),
        vmem((2, 4, rows, half), BF16),
        vmem((half, 4 * rows), BF16),
        vmem((4, rows, width), BF16),
        vmem((4, rows, width), BF16),
        vmem((4, rows, rows), F32),
        vmem((4, rows, rows), F32),
        vmem((3, 4 * rows, half // 3), F32),
        vmem((width + 8, half), F32),
    ]
    for n in range(4):
        count = nz if n < 2 else nz // 2
        scratch += [
            vmem((2, nx, count, 16, half), BF16),
            vmem((nx, count, 16, half), BF16),
            vmem((nx, count, 16, half), BF16),
            vmem((nx, count, 16, half), BF16),
            vmem((count, 16, half), BF16),
            vmem((2 * nz, 16, half), BF16),
            vmem((2, 16, half), BF16),
        ]
    for _ in range(2):
        scratch += [
            vmem((2, 2, rows, rows), BF16),
            vmem((2, rows, rows), BF16),
            vmem((2, rows, rows), BF16),
            vmem((2, rows, rows), BF16),
            vmem((2, 2, rows, rows), BF16),
        ]
    scratch += [sem((7,)), sem((4,)), sem((4,)), sem((4,)), sem((16,)), sem((16,)), sem((6,)), sem((6,))]
    anywhere = pl.BlockSpec(memory_space=pl.ANY)
    return pl.pallas_call(
        functools.partial(mega, nz, nx),
        out_shape=(
            jax.ShapeDtypeStruct((4, rows, width), BF16),
            jax.ShapeDtypeStruct((4, rows, width), BF16),
            jax.ShapeDtypeStruct((2, 2, rows, rows), BF16),
            jax.ShapeDtypeStruct((2, 2, rows, rows), BF16),
            jax.ShapeDtypeStruct((3, 16, width), F32),
        ),
        in_specs=[anywhere] * 7,
        out_specs=(anywhere,) * 4 + (pl.BlockSpec(memory_space=vmem),),
        scratch_shapes=scratch,
        compiler_params=pltpu.CompilerParams(
            collective_id=0, has_side_effects=True, vmem_limit_bytes=60 * 2**20
        ),
        cost_estimate=pl.CostEstimate(
            flops=14 * 10**9, bytes_accessed=16 * 10**6, transcendentals=10**6
        ),
        name="mixing",
    )(*args)


def shards(
    nz, nx, tokens, first_factor, second_factor, value_weight, gate_weight, out_weight, cotangent
):
    rows, width = 4 * nz * nx, 12 * nz * nx
    result, grad, first, second, weights = mega_call(
        nz,
        nx,
        tokens.reshape(4, rows, width),
        first_factor,
        second_factor,
        value_weight,
        gate_weight,
        out_weight,
        cotangent.reshape(4, rows, width),
    )
    return (
        result.reshape(1, 4 * rows, width),
        grad.reshape(1, 4 * rows, width),
        first.astype(F32).reshape(4, rows, rows),
        second.astype(F32).reshape(4, rows, rows),
        weights[0, :12],
        weights[1, :12],
        weights[2, :12],
    )


def solution(mesh, nz=NZ, nx=NX):
    return jax.shard_map(
        functools.partial(shards, nz, nx),
        mesh=mesh,
        in_specs=(
            P("dp", "seq", None),
            P("seq", None, None),
            P("seq", None, None),
            P(),
            P(),
            P(),
            P("dp", "seq", None),
        ),
        out_specs=(
            P("dp", "seq", None),
            P("dp", "seq", None),
            P("seq", None, None),
            P("seq", None, None),
            P("seq", None),
            P("seq", None),
            P("seq", None),
        ),
        check_vma=False,
    )
```

```python
import functools

import jax
import jax.numpy as jnp
from jax import lax
from jax.experimental import pallas as pl
from jax.experimental.pallas import tpu as pltpu
from jax.sharding import PartitionSpec as P

MESH = pl.DeviceIdType.MESH
BF16 = jnp.bfloat16
F32 = jnp.float32
NZ, NX = 4, 16


def dot(left, right):
    return jnp.dot(left, right, preferred_element_type=F32)


def dot_cols(left, right):
    return lax.dot_general(left, right, (((1,), (1,)), ((), ())), preferred_element_type=F32)


def each(count, body):
    def step(i, carry):
        body(i)
        return carry

    lax.fori_loop(0, count, step, 0)


def mega(nz, nx, *refs):
    ns = nz * nx
    rows = 4 * ns
    width = 12 * ns
    half = width // 2
    lanes = half // 3
    (tok_h, ff_h, sf_h, vw_h, gw_h, ow_h, cot_h), refs = refs[:7], refs[7:]
    (res_h, grad_h, first_out, second_out, w_out), refs = refs[:5], refs[5:]
    (tok, ff, sf, vw, gw, ow, cot, tok_t, ff_t, sf_t), refs = refs[:10], refs[10:]
    bsend, brecv, fsend, frecv = (refs[3 * i : 3 * i + 3] for i in range(4))
    refs = refs[12:]
    (bs, val, sig, mix), refs = refs[:4], refs[4:]
    (tmp, got, dval, dgate, sec, sec_t, res, grad), refs = refs[:8], refs[8:]
    (first, second, term, wide), refs = refs[:4], refs[4:]
    jobs = [refs[7 * n : 7 * n + 7] for n in range(4)]
    refs = refs[28:]
    facs = [refs[5 * n : 5 * n + 5] for n in range(2)]
    refs = refs[10:]
    load_sem, store_sem, a2a_send, a2a_recv, job_send, job_recv, fac_send, fac_recv = refs
    a2a, job, fac = (a2a_send, a2a_recv), (job_send, job_recv), (fac_send, fac_recv)

    dp, seq = lax.axis_index("dp"), lax.axis_index("seq")
    zl, core = dp // 2, lax.rem(dp, 2)
    zh, xy = seq // nx, lax.rem(seq, nx)
    z = zh * 2 + zl
    other = 1 - core
    partner = (zl * 2 + other, seq)
    neighbour = ((1 - zl) * 2 + core, seq)

    loads = [
        pltpu.make_async_copy(src, dst, load_sem.at[i])
        for i, (src, dst) in enumerate(
            ((sf_h, sf), (cot_h, cot), (ow_h, ow), (tok_h, tok), (vw_h, vw), (gw_h, gw), (ff_h, ff))
        )
    ]
    for load in loads[:3]:
        load.start()

    barrier = pltpu.get_barrier_semaphore()

    far = sorted(range(1, nz), key=lambda dz: abs(dz - nz / 2))

    def greet(device):
        pl.semaphore_signal(barrier, inc=1, device_id=device, device_id_type=MESH)

    def greet_row(i):
        to_xy = lax.rem(xy + i, nx)
        for dz in far:
            greet((dp, lax.rem(zh + dz, nz) * nx + to_xy))

        @pl.when(i > 0)
        def _():
            greet((dp, zh * nx + to_xy))

    def greet_column(i):
        for d in range(1, 4):
            greet((lax.rem(dp + d, 4), i * nx + xy))

    each(nx, greet_row)
    each(nz, greet_column)

    def remote(src, dst, sems, k, device):
        return pltpu.make_async_remote_copy(
            src_ref=src,
            dst_ref=dst,
            send_sem=sems[0].at[k],
            recv_sem=sems[1].at[k],
            device_id=device,
            device_id_type=MESH,
        )

    def send_all(src, dst, k):
        def send(to):
            remote(src.at[to], dst.at[seq], a2a, k, (dp, to)).start()

        def row(i):
            for dz in far:
                send(lax.rem(zh + dz, nz) * nx + lax.rem(xy + i, nx))

        each(nx, row)
        each(nx - 1, lambda i: send(zh * nx + lax.rem(xy + i + 1, nx)))
        dst[seq] = src[seq]

    def all_of(src, dst, k):
        some = pl.ds(0, ns - 1)
        return remote(src.at[some], dst.at[some], a2a, k, (dp, lax.rem(seq + 1, ns)))

    def to_messages(dst, start, size):
        tiles = min(8, rows // 8)
        mask = lax.broadcasted_iota(jnp.int32, (tiles, 8, size), 1) < 4

        def block(i):
            at = pl.ds(pl.multiple_of(i * tiles * 8, 8), tiles * 8)
            r = [tmp[k, at, start : start + size].reshape(tiles, 8, size) for k in range(4)]
            turned = [pltpu.roll(x, 4, 1) for x in r]
            low = [jnp.where(mask, r[k], turned[k + 1]) for k in (0, 2)]
            high = [jnp.where(mask, turned[k], r[k + 1]) for k in (0, 2)]
            low = jnp.concatenate(low, axis=1).astype(BF16)
            high = jnp.concatenate(high, axis=1).astype(BF16)
            for t in range(tiles):
                dst[(i * tiles + t) * 2] = low[t]
                dst[(i * tiles + t) * 2 + 1] = high[t]

        each(rows // (tiles * 8), block)

    def from_messages(src, start, size):
        for j in range(size // lanes):
            cols = slice(j * lanes, (j + 1) * lanes)
            to_cols = slice(start + j * lanes, start + (j + 1) * lanes)

            def widen(i, j=j, cols=cols):
                at = pl.ds(pl.multiple_of(i * 64, 64), 64)
                part = src[pl.ds(i * 4, 4), :, cols]
                term[j, at, :] = part.reshape(64, lanes).astype(F32)

            each(4 * rows // 64, widen)
            for k in range(4):
                got[k, :, to_cols] = term[j, pl.ds(k, rows, stride=4), :].astype(BF16)

    def zone(n):
        count = nz if n < 2 else nz // 2
        base = 0 if n < 2 else (n - 2) * count
        inside = (zh >= base) & (zh < base + count)
        return count, base, inside, inside & (zl == n % 2)

    def put_rows(n, which, first_pair, last_pair):
        own = jobs[n][0]

        def two(i):
            m = first_pair + i
            x = wide[which, pl.ds(pl.multiple_of(24 * m, 8), 32), :]
            for k in range(2):
                s = 2 * m + k
                block = x[12 * k : 12 * k + 16].astype(BF16)
                own[which, lax.rem(s, nx), s // nx] = block

        each(last_pair - first_pair, two)

    def pair_copy(n):
        return remote(jobs[n][0].at[other], jobs[n][1], job, 4 * n, partner)

    def pair_add(n):
        own, pair, u, plane = jobs[n][:4]
        pair_copy(n).wait()

        def add(i):
            u[i] = (own[core, i].astype(F32) + pair[i].astype(F32)).astype(BF16)

        each(nx, add)

        def send(i):
            to = lax.rem(xy + i + 1, nx)
            remote(u.at[to], plane.at[xy], job, 4 * n + 1, (dp, zh * nx + to)).start()

        each(nx - 1, send)
        plane[xy] = u[xy]

    def plane_add(n):
        u, plane, total, col = jobs[n][2:6]
        count, base, inside, member = zone(n)
        remote(
            u.at[pl.ds(0, nx - 1)], plane.at[pl.ds(0, nx - 1)], job, 4 * n + 1, partner
        ).wait()

        def add(q):
            x = plane[0, q].astype(F32)
            for i in range(1, nx):
                x = x + plane[i, q].astype(F32)
            total[q] = x.astype(BF16)

        each(count, add)
        if n < 3:

            def send(i):
                @pl.when((base + i != zh) | (zl != n % 2))
                def _():
                    device = ((n % 2) * 2 + core, (base + i) * nx + xy)
                    remote(total.at[i], col.at[z], job, 4 * n + 2, device).start()

            each(count, send)

            @pl.when(member)
            def _():
                col[z] = total[zh - base]

        else:

            def send(i):
                to_dp = lax.rem(i, 4)

                @pl.when((base + i // 4 != zh) | (to_dp != dp))
                def _():
                    device = (to_dp, (base + i // 4) * nx + xy)
                    slot = col.at[core * 2 * nz + z]
                    remote(total.at[i // 4], slot, job, 4 * n + 2, device).start()

            each(4 * count, send)

            @pl.when(inside)
            def _():
                col[core * 2 * nz + z] = total[zh - base]

    def pieces(n, sem, size):
        some = pl.ds(0, size)
        return remote(jobs[n][5].at[some], jobs[n][5].at[some], job, 4 * n + sem, partner)

    def sum_of(col, start):
        x = col[start].astype(F32)
        for i in range(1, 2 * nz):
            x = x + col[start + i].astype(F32)
        return x

    def column_add(n):
        col, fin = jobs[n][5:]
        count, _, _, member = zone(n)

        @pl.when(member)
        def _():
            pieces(n, 2, 2 * nz - 1).wait_recv()
            fin[core] = sum_of(col, 0).astype(BF16)
            for d in range(1, 4):
                device = (lax.rem(dp + d, 4), seq)
                remote(fin.at[core], fin.at[core], job, 4 * n + 3, device).start()
            pieces(n, 2, count - 1).wait_send()

        @pl.when(jnp.logical_not(member))
        def _():
            pieces(n, 2, count).wait_send()

    def finish(n):
        fin = jobs[n][6]
        _, _, inside, member = zone(n)

        @pl.when(inside)
        def _():
            @pl.when(member)
            def _():
                remote(fin.at[other], fin.at[other], job, 4 * n + 3, partner).wait_recv()
                pieces(n, 3, 3).wait_send()

            @pl.when(jnp.logical_not(member))
            def _():
                remote(fin, fin, job, 4 * n + 3, partner).wait_recv()

            at = [
                ((0, slice(0, half)), (1, slice(0, half))),
                ((0, slice(half, width)), (1, slice(half, width))),
                ((2, slice(0, half)), (2, slice(half, width))),
            ][n]
            for k in range(2):
                w_out[at[k][0], :, at[k][1]] = fin[k].astype(F32)

    def finish_last():
        col = jobs[3][5]
        count, _, inside, _ = zone(3)

        @pl.when(inside)
        def _():
            pieces(3, 2, 4 * nz - 1).wait_recv()
            for k in range(2):
                total = sum_of(col, 2 * nz * k).astype(BF16)
                w_out[2, :, k * half : (k + 1) * half] = total.astype(F32)
            pieces(3, 2, 4 * count - 1).wait_send()

        @pl.when(jnp.logical_not(inside))
        def _():
            pieces(3, 2, 4 * count).wait_send()

    def factor_start(n, source):
        own, pair = facs[n][:2]
        for k in range(4):
            own[k // 2, k % 2] = source[k].astype(BF16)
        remote(own.at[other], pair, fac, 5 * n, partner).start()

    def factor_pair(n):
        own, pair, u = facs[n][:3]
        remote(own.at[other], pair, fac, 5 * n, partner).wait()
        for k in range(2):
            u[k] = (own[core, k].astype(F32) + pair[k].astype(F32)).astype(BF16)

    def near_copy(n, k):
        return remote(facs[n][2].at[k], facs[n][3].at[k], fac, 5 * n + 1 + k, neighbour)

    def fin_copy(n, k):
        fin = facs[n][4]
        return remote(fin.at[core, k], fin.at[core, k], fac, 5 * n + 3 + k, partner)

    def factor_near(n):
        _, _, u, near, fin = facs[n]
        for k in range(2):
            near_copy(n, k).wait()
            fin[core, k] = (u[k].astype(F32) + near[k].astype(F32)).astype(BF16)
            fin_copy(n, k).start()

    def factor_end(n, wide_sum, store):
        fin = facs[n][4]
        for k in range(2):
            fin_copy(n, k).wait()
        for k in range(4):
            wide_sum[k] = fin[k // 2, k % 2].astype(F32)
        store.start()

    stores = [
        pltpu.make_async_copy(src, dst, store_sem.at[i])
        for i, (src, dst) in enumerate(
            ((res, res_h), (grad, grad_h), (first, first_out), (second, second_out))
        )
    ]
    for which in range(2):
        wide[which, width:, :] = jnp.zeros((8, half), F32)

    loads[0].wait()
    for k in range(4):
        sf_t[k] = sf[k].T
    loads[1].wait()
    loads[2].wait()
    for load in loads[3:]:
        load.start()
    back_groups = ((0, 0, lanes), (0, lanes, 2 * lanes), (1, 0, half))
    for g, (c, start, size) in enumerate(back_groups):

        def back(p, c=c, start=start, size=size):
            at = c * half + start
            part = dot_cols(cot[p], ow[at : at + size, :]).astype(BF16)
            bs[c, p, :, start : start + size] = part
            tmp[p, :, :size] = dot(sf_t[p], part)

        each(4, back)
        to_messages(bsend[g], 0, size)
        if g == 0:
            pl.semaphore_wait(barrier, ns - 1 + 3 * nz)
        send_all(bsend[g], brecv[g], g)

    for load in loads[3:]:
        load.wait()
    forward_groups = ((0, 0, half), (1, 0, 2 * lanes), (1, 2 * lanes, lanes))
    for c in range(2):
        cols = slice(c * half, (c + 1) * half)

        def forward(a, c=c, cols=cols):
            v = dot(tok[a], vw[:, cols])
            s = jax.nn.sigmoid(dot(tok[a], gw[:, cols]))
            m = (v * s).astype(BF16)
            val[c, a] = v
            sig[c, a] = s
            mix[c, a] = m
            tmp[a] = dot(ff[a], m)

        each(4, forward)
        for g, (group_c, start, size) in enumerate(forward_groups):
            if group_c == c:
                to_messages(fsend[g], start, size)
    for k in range(4):
        ff_t[k] = ff[k].T
        tok_t[:, k * rows : (k + 1) * rows] = tok[k].T

    def back_copy(g):
        return all_of(bsend[g], brecv[g], g)

    def forward_copy(g):
        return all_of(fsend[g], frecv[g], 3 + g)

    for c in range(2):
        groups = [g for g in range(3) if back_groups[g][0] == c]
        for g in groups:
            back_copy(g).wait_send()
        for g in range(3):
            if forward_groups[g][0] == c:
                send_all(fsend[g], frecv[g], 3 + g)
        for g in groups:
            back_copy(g).wait_recv()
            from_messages(brecv[g], *back_groups[g][1:])

        def inner(a, c=c):
            g = got[a]
            part = dot(ff_t[a], g)
            s = sig[c, a]
            ps = part * s
            dval[c, a] = ps.astype(BF16)
            dgate[c, a] = (ps * val[c, a] * (1.0 - s)).astype(BF16)
            more = dot_cols(g, mix[c, a])
            if c == 0:
                first[a] = more
            else:
                first[a] = first[a] + more

        each(4, inner)
        for which, source in enumerate((dval, dgate)):

            def terms(m, c=c, which=which, source=source):
                at = pl.ds(pl.multiple_of(m * rows, 8), rows)
                wide[which, at, :] = dot(tok_t[at, :], source[c].reshape(4 * rows, half))

            each(3, terms)
            put_rows(c, which, 0, ns // 2)
        pair_copy(c).start()
    factor_start(0, first)
    pair_add(0)
    pair_add(1)
    factor_pair(0)
    near_copy(0, 0).start()

    def grads(a):
        x = dot_cols(dval[0, a], vw[:, :half]) + dot_cols(dval[1, a], vw[:, half:])
        y = dot_cols(dgate[0, a], gw[:, :half]) + dot_cols(dgate[1, a], gw[:, half:])
        grad[a] = (x + y).astype(BF16)

    each(4, grads)
    stores[1].start()

    def mix_second(g):
        c, start, size = forward_groups[g]
        cols = slice(start, start + size)
        forward_copy(g).wait_recv()
        from_messages(frecv[g], start, size)

        def inner(p):
            sec[c, p, :, cols] = dot(sf[p], got[p, :, cols]).astype(BF16)

        each(4, inner)
        for k in range(4):
            sec_t[cols, k * rows : (k + 1) * rows] = sec[c, k, :, cols].T
        for which in range(2):
            right = cot[:, :, which * half : (which + 1) * half].reshape(4 * rows, half)
            wide[which, cols, :] = dot(sec_t[cols, :], right)

    def grow_second(g):
        c, start, size = forward_groups[g]
        cols = slice(start, start + size)

        def outer(p):
            more = dot_cols(bs[c, p, :, cols], got[p, :, cols])
            if g == 0:
                second[p] = more
            else:
                second[p] = second[p] + more

        each(4, outer)

    early = 2 * lanes // 24
    mix_second(0)
    for which in range(2):
        put_rows(2, which, 0, ns // 4)
    pair_copy(2).start()
    grow_second(0)
    plane_add(0)
    plane_add(1)
    pair_add(2)
    mix_second(1)
    for which in range(2):
        put_rows(3, which, 0, early)
    grow_second(1)
    for g in range(3):
        forward_copy(g).wait_send()
    near_copy(0, 1).start()
    mix_second(2)
    for which in range(2):
        put_rows(3, which, early, ns // 4)
    pair_copy(3).start()
    grow_second(2)
    factor_start(1, second)
    pair_add(3)
    factor_pair(1)
    for k in range(2):
        near_copy(1, k).start()
    column_add(0)
    column_add(1)
    plane_add(2)
    factor_near(0)

    def results(p):
        x = dot(sec[0, p], ow[:half, :]) + dot(sec[1, p], ow[half:, :])
        res[p] = x.astype(BF16)

    each(4, results)
    stores[0].start()
    plane_add(3)
    factor_end(0, first, stores[2])
    column_add(2)
    for n in range(2):
        finish(n)
    factor_near(1)
    finish(2)
    finish_last()
    factor_end(1, second, stores[3])
    for store in stores:
        store.wait()


def mega_call(nz, nx, *args):
    ns = nz * nx
    rows = 4 * ns
    width = 12 * ns
    half = width // 2
    vmem, sem = pltpu.VMEM, pltpu.SemaphoreType.DMA
    scratch = [
        vmem((4, rows, width), BF16),
        vmem((4, rows, rows), BF16),
        vmem((4, rows, rows), BF16),
        vmem((width, width), BF16),
        vmem((width, width), BF16),
        vmem((width, width), BF16),
        vmem((4, rows, width), BF16),
        vmem((width, 4 * rows), BF16),
        vmem((4, rows, rows), BF16),
        vmem((4, rows, rows), BF16),
    ]
    for sizes in ((1, 2, 3), (1, 2, 3), (3, 2, 1), (3, 2, 1)):
        scratch += [vmem((ns, 16, half // 3 * size), BF16) for size in sizes]
    scratch += [
        vmem((2, 4, rows, half), BF16),
        vmem((2, 4, rows, half), F32),
        vmem((2, 4, rows, half), F32),
        vmem((2, 4, rows, half), BF16),
        vmem((4, rows, half), F32),
        vmem((4, rows, half), BF16),
        vmem((2, 4, rows, half), BF16),
        vmem((2, 4, rows, half), BF16),
        vmem((2, 4, rows, half), BF16),
        vmem((half, 4 * rows), BF16),
        vmem((4, rows, width), BF16),
        vmem((4, rows, width), BF16),
        vmem((4, rows, rows), F32),
        vmem((4, rows, rows), F32),
        vmem((3, 4 * rows, half // 3), F32),
        vmem((2, width + 8, half), F32),
    ]
    for n in range(4):
        count = nz if n < 2 else nz // 2
        scratch += [
            vmem((2, nx, count, 16, half), BF16),
            vmem((nx, count, 16, half), BF16),
            vmem((nx, count, 16, half), BF16),
            vmem((nx, count, 16, half), BF16),
            vmem((count, 16, half), BF16),
            vmem((4 * nz if n == 3 else 2 * nz, 16, half), BF16),
            vmem((2, 16, half), BF16),
        ]
    for _ in range(2):
        scratch += [
            vmem((2, 2, rows, rows), BF16),
            vmem((2, rows, rows), BF16),
            vmem((2, rows, rows), BF16),
            vmem((2, rows, rows), BF16),
            vmem((2, 2, rows, rows), BF16),
        ]
    scratch += [sem((count,)) for count in (7, 4, 6, 6, 16, 16, 10, 10)]
    anywhere = pl.BlockSpec(memory_space=pl.ANY)
    return pl.pallas_call(
        functools.partial(mega, nz, nx),
        out_shape=(
            jax.ShapeDtypeStruct((4, rows, width), BF16),
            jax.ShapeDtypeStruct((4, rows, width), BF16),
            jax.ShapeDtypeStruct((4, rows, rows), F32),
            jax.ShapeDtypeStruct((4, rows, rows), F32),
            jax.ShapeDtypeStruct((3, 16, width), F32),
        ),
        in_specs=[anywhere] * 7,
        out_specs=(anywhere,) * 4 + (pl.BlockSpec(memory_space=vmem),),
        scratch_shapes=scratch,
        compiler_params=pltpu.CompilerParams(
            collective_id=0, has_side_effects=True, vmem_limit_bytes=60 * 2**20
        ),
        cost_estimate=pl.CostEstimate(
            flops=14 * 10**9, bytes_accessed=16 * 10**6, transcendentals=10**6
        ),
        name="mixing",
    )(*args)


def deliver(*refs):
    sources, weights, targets, parts, sem = refs[:4], refs[4], refs[5:9], refs[9:12], refs[12]
    copies = [
        pltpu.make_async_copy(src.at[i], dst.at[i], sem.at[4 * n + i])
        for n, (src, dst) in enumerate(zip(sources, targets))
        for i in range(4)
    ]
    for copy in copies:
        copy.start()
    for i in range(3):
        parts[i][...] = weights[i, :12, :]
    for copy in copies:
        copy.wait()


def deliver_call(*arrays):
    anywhere, vmem = pl.BlockSpec(memory_space=pl.ANY), pl.BlockSpec(memory_space=pltpu.VMEM)
    small = jax.ShapeDtypeStruct((12, arrays[4].shape[2]), F32)
    return pl.pallas_call(
        deliver,
        out_shape=tuple(jax.ShapeDtypeStruct(x.shape, x.dtype) for x in arrays[:4]) + (small,) * 3,
        in_specs=[anywhere] * 4 + [vmem],
        out_specs=(anywhere,) * 4 + (vmem,) * 3,
        scratch_shapes=[pltpu.SemaphoreType.DMA((16,))],
        name="deliver",
    )(*arrays)


def shards(
    nz, nx, tokens, first_factor, second_factor, value_weight, gate_weight, out_weight, cotangent
):
    rows, width = 4 * nz * nx, 12 * nz * nx
    arrays = mega_call(
        nz,
        nx,
        tokens.reshape(4, rows, width),
        first_factor,
        second_factor,
        value_weight,
        gate_weight,
        out_weight,
        cotangent.reshape(4, rows, width),
    )
    result, grad, first, second, value_sum, gate_sum, out_sum = deliver_call(*arrays)
    return (
        result.reshape(1, 4 * rows, width),
        grad.reshape(1, 4 * rows, width),
        first,
        second,
        value_sum,
        gate_sum,
        out_sum,
    )


def solution(mesh, nz=NZ, nx=NX):
    return jax.shard_map(
        functools.partial(shards, nz, nx),
        mesh=mesh,
        in_specs=(
            P("dp", "seq", None),
            P("seq", None, None),
            P("seq", None, None),
            P(),
            P(),
            P(),
            P("dp", "seq", None),
        ),
        out_specs=(
            P("dp", "seq", None),
            P("dp", "seq", None),
            P("seq", None, None),
            P("seq", None, None),
            P("seq", None),
            P("seq", None),
            P("seq", None),
        ),
        check_vma=False,
    )
```

```python
import functools

import jax
import jax.numpy as jnp
from jax import lax
from jax.experimental import pallas as pl
from jax.experimental.pallas import tpu as pltpu
from jax.sharding import PartitionSpec as P

MESH = pl.DeviceIdType.MESH
BF16 = jnp.bfloat16
F32 = jnp.float32
NZ, NX = 4, 16


def dot(left, right):
    return jnp.dot(left, right, preferred_element_type=F32)


def dot_cols(left, right):
    return lax.dot_general(left, right, (((1,), (1,)), ((), ())), preferred_element_type=F32)


def each(count, body):
    def step(i, carry):
        body(i)
        return carry

    lax.fori_loop(0, count, step, 0)


def zone_of(nz, n):
    return ((nz, 0), (nz, 0), (nz // 2, 0), (nz // 4, nz // 2), (nz // 4, 3 * nz // 4))[n]


def mega(nz, nx, *refs):
    ns = nz * nx
    rows = 4 * ns
    width = 12 * ns
    half = width // 2
    lanes = half // 3
    (tok_h, ff_h, sf_h, vw_h, gw_h, ow_h, cot_h), refs = refs[:7], refs[7:]
    (res_h, grad_h, first_out, second_out), w_out, refs = refs[:4], refs[4:7], refs[7:]
    (tok, ff, sf, vw, gw, ow, cot, tok_t, ff_t, sf_t), refs = refs[:10], refs[10:]
    bsend, brecv, fsend, frecv = (refs[3 * i : 3 * i + 3] for i in range(4))
    refs = refs[12:]
    (bs, val, sig, mix), refs = refs[:4], refs[4:]
    (tmp, got, dval, dgate, sec, sec_t, res, grad), refs = refs[:8], refs[8:]
    (first, second, term, wide), refs = refs[:4], refs[4:]
    jobs = [refs[7 * n : 7 * n + 7] for n in range(5)]
    refs = refs[35:]
    facs = [refs[5 * n : 5 * n + 5] for n in range(2)]
    refs = refs[10:]
    load_sem, store_sem, a2a_send, a2a_recv, job_send, job_recv, fac_send, fac_recv = refs
    a2a, job, fac = (a2a_send, a2a_recv), (job_send, job_recv), (fac_send, fac_recv)

    dp, seq = lax.axis_index("dp"), lax.axis_index("seq")
    zl, core = dp // 2, lax.rem(dp, 2)
    zh, xy = seq // nx, lax.rem(seq, nx)
    z = zh * 2 + zl
    other = 1 - core
    partner = (zl * 2 + other, seq)
    neighbour = ((1 - zl) * 2 + core, seq)

    back_groups = ((0, 0, lanes), (0, lanes, 2 * lanes), (1, 0, half))
    parts = [(sf_h, sf)]
    for c, start, size in back_groups:
        at = pl.ds(c * half + start, size)
        parts.append((ow_h.at[at, :], ow.at[at, :]))
    parts += [(cot_h.at[p], cot.at[p]) for p in range(4)]
    parts += [(tok_h, tok), (vw_h, vw), (gw_h, gw), (ff_h, ff)]
    loads = [
        pltpu.make_async_copy(src, dst, load_sem.at[i]) for i, (src, dst) in enumerate(parts)
    ]
    for i in (0, 1, 4, 5, 6, 7, 2, 3):
        loads[i].start()

    barrier = pltpu.get_barrier_semaphore()

    far = sorted(range(1, nz), key=lambda dz: abs(dz - nz / 2))

    def greet(device):
        pl.semaphore_signal(barrier, inc=1, device_id=device, device_id_type=MESH)

    def greet_row(i):
        to_xy = lax.rem(xy + i, nx)
        for dz in far:
            greet((dp, lax.rem(zh + dz, nz) * nx + to_xy))

        @pl.when(i > 0)
        def _():
            greet((dp, zh * nx + to_xy))

    def greet_column(i):
        for d in range(1, 4):
            greet((lax.rem(dp + d, 4), i * nx + xy))

    each(nx, greet_row)
    each(nz, greet_column)

    def remote(src, dst, sems, k, device):
        return pltpu.make_async_remote_copy(
            src_ref=src,
            dst_ref=dst,
            send_sem=sems[0].at[k],
            recv_sem=sems[1].at[k],
            device_id=device,
            device_id_type=MESH,
        )

    def send_all(src, dst, k):
        def send(to):
            remote(src.at[to], dst.at[seq], a2a, k, (dp, to)).start()

        def row(i):
            for dz in far:
                send(lax.rem(zh + dz, nz) * nx + lax.rem(xy + i, nx))

        each(nx, row)
        each(nx - 1, lambda i: send(zh * nx + lax.rem(xy + i + 1, nx)))
        dst[seq] = src[seq]

    def all_of(src, dst, k):
        some = pl.ds(0, ns - 1)
        return remote(src.at[some], dst.at[some], a2a, k, (dp, lax.rem(seq + 1, ns)))

    def to_messages(dst, start, size):
        tiles = min(8, rows // 8)
        mask = lax.broadcasted_iota(jnp.int32, (tiles, 8, size), 1) < 4

        def block(i):
            at = pl.ds(pl.multiple_of(i * tiles * 8, 8), tiles * 8)
            r = [tmp[k, at, start : start + size].reshape(tiles, 8, size) for k in range(4)]
            turned = [pltpu.roll(x, 4, 1) for x in r]
            low = [jnp.where(mask, r[k], turned[k + 1]) for k in (0, 2)]
            high = [jnp.where(mask, turned[k], r[k + 1]) for k in (0, 2)]
            low = jnp.concatenate(low, axis=1).astype(BF16)
            high = jnp.concatenate(high, axis=1).astype(BF16)
            for t in range(tiles):
                dst[(i * tiles + t) * 2] = low[t]
                dst[(i * tiles + t) * 2 + 1] = high[t]

        each(rows // (tiles * 8), block)

    def from_messages(src, start, size):
        for j in range(size // lanes):
            cols = slice(j * lanes, (j + 1) * lanes)
            to_cols = slice(start + j * lanes, start + (j + 1) * lanes)

            def widen(i, j=j, cols=cols):
                at = pl.ds(pl.multiple_of(i * 64, 64), 64)
                part = src[pl.ds(i * 4, 4), :, cols]
                term[j, at, :] = part.reshape(64, lanes).astype(F32)

            each(4 * rows // 64, widen)
            for k in range(4):
                got[k, :, to_cols] = term[j, pl.ds(k, rows, stride=4), :].astype(BF16)

    def zone(n):
        count, base = zone_of(nz, n)
        inside = (zh >= base) & (zh < base + count)
        return count, base, inside, inside & (zl == n % 2)

    def put_rows(n, which, start, stop, offset=0):
        own = jobs[n][0]

        def two(i):
            m = start + i
            x = wide[which, pl.ds(pl.multiple_of(24 * (m + offset), 8), 32), :]
            for k in range(2):
                s = 2 * m + k
                block = x[12 * k : 12 * k + 16].astype(BF16)
                own[which, lax.rem(s, nx), s // nx] = block

        each(stop - start, two)

    def pair_copy(n):
        return remote(jobs[n][0].at[other], jobs[n][1], job, 4 * n, partner)

    def pair_add(n):
        own, pair, u, plane = jobs[n][:4]
        pair_copy(n).wait()

        def add(i):
            u[i] = (own[core, i].astype(F32) + pair[i].astype(F32)).astype(BF16)

        each(nx, add)

        def send(i):
            to = lax.rem(xy + i + 1, nx)
            remote(u.at[to], plane.at[xy], job, 4 * n + 1, (dp, zh * nx + to)).start()

        each(nx - 1, send)
        plane[xy] = u[xy]

    def plane_add(n):
        u, plane, total, col = jobs[n][2:6]
        count, base, inside, member = zone(n)
        remote(
            u.at[pl.ds(0, nx - 1)], plane.at[pl.ds(0, nx - 1)], job, 4 * n + 1, partner
        ).wait()

        def add(q):
            x = plane[0, q].astype(F32)
            for i in range(1, nx):
                x = x + plane[i, q].astype(F32)
            total[q] = x.astype(BF16)

        each(count, add)
        if n < 3:

            def send(i):
                @pl.when((base + i != zh) | (zl != n % 2))
                def _():
                    device = ((n % 2) * 2 + core, (base + i) * nx + xy)
                    remote(total.at[i], col.at[z], job, 4 * n + 2, device).start()

            each(count, send)

            @pl.when(member)
            def _():
                col[z] = total[zh - base]

        else:

            def send(i):
                to_dp = lax.rem(i, 4)

                @pl.when((base + i // 4 != zh) | (to_dp != dp))
                def _():
                    device = (to_dp, (base + i // 4) * nx + xy)
                    slot = col.at[core * 2 * nz + z]
                    remote(total.at[i // 4], slot, job, 4 * n + 2, device).start()

            each(4 * count, send)

            @pl.when(inside)
            def _():
                col[core * 2 * nz + z] = total[zh - base]

    def pieces(n, sem, size):
        some = pl.ds(0, size)
        return remote(jobs[n][5].at[some], jobs[n][5].at[some], job, 4 * n + sem, partner)

    def sum_of(col, start):
        x = col[start].astype(F32)
        for i in range(1, 2 * nz):
            x = x + col[start + i].astype(F32)
        return x

    def column_add(n):
        col, fin = jobs[n][5:]
        count, _, _, member = zone(n)

        @pl.when(member)
        def _():
            pieces(n, 2, 2 * nz - 1).wait_recv()
            fin[core] = sum_of(col, 0).astype(BF16)
            for d in range(1, 4):
                device = (lax.rem(dp + d, 4), seq)
                remote(fin.at[core], fin.at[core], job, 4 * n + 3, device).start()
            pieces(n, 2, count - 1).wait_send()

        @pl.when(jnp.logical_not(member))
        def _():
            pieces(n, 2, count).wait_send()

    def finish(n):
        fin = jobs[n][6]
        _, _, inside, member = zone(n)

        @pl.when(inside)
        def _():
            @pl.when(member)
            def _():
                remote(fin.at[other], fin.at[other], job, 4 * n + 3, partner).wait_recv()
                pieces(n, 3, 3).wait_send()

            @pl.when(jnp.logical_not(member))
            def _():
                remote(fin, fin, job, 4 * n + 3, partner).wait_recv()

            at = [
                ((0, slice(0, half)), (1, slice(0, half))),
                ((0, slice(half, width)), (1, slice(half, width))),
                ((2, slice(0, half)), (2, slice(half, width))),
            ][n]
            for k in range(2):
                w_out[at[k][0]][:, at[k][1]] = fin[k].astype(F32)[:12]

    def finish_last(n):
        col = jobs[n][5]
        count, _, inside, _ = zone(n)

        @pl.when(inside)
        def _():
            pieces(n, 2, 4 * nz - 1).wait_recv()
            for k in range(2):
                total = sum_of(col, 2 * nz * k).astype(BF16)
                w_out[2][:, k * half : (k + 1) * half] = total.astype(F32)[:12]
            pieces(n, 2, 4 * count - 1).wait_send()

        @pl.when(jnp.logical_not(inside))
        def _():
            pieces(n, 2, 4 * count).wait_send()

    def factor_copy(n, k):
        own, pair = facs[n][:2]
        return remote(own.at[other, k], pair.at[k], fac, 6 * n + k, partner)

    def factor_start(n, source):
        own = facs[n][0]
        for k in range(2):
            for h in range(2):
                own[h, k] = source[2 * h + k].astype(BF16)
            factor_copy(n, k).start()

    def factor_pair(n, send):
        own, pair, u = facs[n][:3]
        for k in range(2):
            factor_copy(n, k).wait()
            u[k] = (own[core, k].astype(F32) + pair[k].astype(F32)).astype(BF16)
            if k < send:
                near_copy(n, k).start()

    def near_copy(n, k):
        return remote(facs[n][2].at[k], facs[n][3].at[k], fac, 6 * n + 2 + k, neighbour)

    def fin_copy(n, k):
        fin = facs[n][4]
        return remote(fin.at[core, k], fin.at[core, k], fac, 6 * n + 4 + k, partner)

    def factor_near(n):
        _, _, u, near, fin = facs[n]
        for k in range(2):
            near_copy(n, k).wait()
            fin[core, k] = (u[k].astype(F32) + near[k].astype(F32)).astype(BF16)
            fin_copy(n, k).start()

    def factor_end(n, wide_sum, store):
        fin = facs[n][4]
        for k in range(2):
            fin_copy(n, k).wait()
        for k in range(4):
            wide_sum[k] = fin[k // 2, k % 2].astype(F32)
        store.start()

    stores = [
        pltpu.make_async_copy(src, dst, store_sem.at[i])
        for i, (src, dst) in enumerate(
            ((res, res_h), (grad, grad_h), (first, first_out), (second, second_out))
        )
    ]
    for which in range(2):
        wide[which, width:, :] = jnp.zeros((8, half), F32)

    for g, (c, start, size) in enumerate(back_groups):
        loads[1 + g].wait()

        def back(p, c=c, start=start, size=size):
            at = c * half + start
            part = dot_cols(cot[p], ow[at : at + size, :]).astype(BF16)
            bs[c, p, :, start : start + size] = part
            tmp[p, :, :size] = dot(sf_t[p], part)

        if g == 0:
            loads[0].wait()
            for p in range(4):
                sf_t[p] = sf[p].T
                loads[4 + p].wait()
                back(p)
            for load in loads[8:]:
                load.start()
        else:
            each(4, back)
        to_messages(bsend[g], 0, size)
        if g == 0:
            pl.semaphore_wait(barrier, ns - 1 + 3 * nz)
        send_all(bsend[g], brecv[g], g)

    for load in loads[8:]:
        load.wait()
    forward_groups = ((0, 0, half), (1, 0, 2 * lanes), (1, 2 * lanes, lanes))
    for c in range(2):
        cols = slice(c * half, (c + 1) * half)

        def forward(a, c=c, cols=cols):
            v = dot(tok[a], vw[:, cols])
            s = jax.nn.sigmoid(dot(tok[a], gw[:, cols]))
            m = (v * s).astype(BF16)
            val[c, a] = v
            sig[c, a] = s
            mix[c, a] = m
            tmp[a] = dot(ff[a], m)

        each(4, forward)
        for g, (group_c, start, size) in enumerate(forward_groups):
            if group_c == c:
                to_messages(fsend[g], start, size)
    for k in range(4):
        ff_t[k] = ff[k].T
        tok_t[:, k * rows : (k + 1) * rows] = tok[k].T

    def back_copy(g):
        return all_of(bsend[g], brecv[g], g)

    def forward_copy(g):
        return all_of(fsend[g], frecv[g], 3 + g)

    for c in range(2):
        groups = [g for g in range(3) if back_groups[g][0] == c]
        for g in groups:
            back_copy(g).wait_send()
        for g in range(3):
            if forward_groups[g][0] == c:
                send_all(fsend[g], frecv[g], 3 + g)
        if c == 1:
            pair_add(0)
        for g in groups:
            back_copy(g).wait_recv()
            from_messages(brecv[g], *back_groups[g][1:])

        def inner(a, c=c):
            g = got[a]
            part = dot(ff_t[a], g)
            s = sig[c, a]
            ps = part * s
            dval[c, a] = ps.astype(BF16)
            dgate[c, a] = (ps * val[c, a] * (1.0 - s)).astype(BF16)
            more = dot_cols(g, mix[c, a])
            if c == 0:
                first[a] = more
            else:
                first[a] = first[a] + more

        each(4, inner)
        for which, source in enumerate((dval, dgate)):

            def terms(m, c=c, which=which, source=source):
                at = pl.ds(pl.multiple_of(m * rows, 8), rows)
                wide[which, at, :] = dot(tok_t[at, :], source[c].reshape(4 * rows, half))

            each(3, terms)
            put_rows(c, which, 0, ns // 2)
        pair_copy(c).start()
    factor_start(0, first)
    pair_add(1)
    factor_pair(0, 1)

    def grads(a):
        x = dot_cols(dval[0, a], vw[:, :half]) + dot_cols(dval[1, a], vw[:, half:])
        y = dot_cols(dgate[0, a], gw[:, :half]) + dot_cols(dgate[1, a], gw[:, half:])
        grad[a] = (x + y).astype(BF16)

    each(4, grads)
    stores[1].start()
    plane_add(0)

    def mix_second(g):
        c, start, size = forward_groups[g]
        cols = slice(start, start + size)
        forward_copy(g).wait_recv()
        from_messages(frecv[g], start, size)

        def inner(p):
            sec[c, p, :, cols] = dot(sf[p], got[p, :, cols]).astype(BF16)

        each(4, inner)
        for k in range(4):
            sec_t[cols, k * rows : (k + 1) * rows] = sec[c, k, :, cols].T
        for which in range(2):
            right = cot[:, :, which * half : (which + 1) * half].reshape(4 * rows, half)
            wide[which, cols, :] = dot(sec_t[cols, :], right)

    def grow_second(g):
        c, start, size = forward_groups[g]
        cols = slice(start, start + size)

        def outer(p):
            more = dot_cols(bs[c, p, :, cols], got[p, :, cols])
            if g == 0:
                second[p] = more
            else:
                second[p] = second[p] + more

        each(4, outer)

    mix_second(0)
    for which in range(2):
        put_rows(2, which, 0, ns // 4)
    pair_copy(2).start()
    grow_second(0)
    plane_add(1)
    pair_add(2)
    pairs = ns // 8
    early = 2 * lanes // 24 - pairs
    mix_second(1)
    for which in range(2):
        put_rows(3, which, 0, pairs)
    pair_copy(3).start()
    for which in range(2):
        put_rows(4, which, 0, early, pairs)
    grow_second(1)
    pair_add(3)
    for g in range(3):
        forward_copy(g).wait_send()
    near_copy(0, 1).start()
    plane_add(2)
    column_add(0)
    column_add(1)
    mix_second(2)
    for which in range(2):
        put_rows(4, which, early, pairs, pairs)
    pair_copy(4).start()
    grow_second(2)
    factor_start(1, second)
    pair_add(4)
    factor_pair(1, 2)
    plane_add(3)
    factor_near(0)

    def results(p):
        x = dot(sec[0, p], ow[:half, :]) + dot(sec[1, p], ow[half:, :])
        res[p] = x.astype(BF16)

    each(4, results)
    stores[0].start()
    factor_end(0, first, stores[2])
    plane_add(4)
    column_add(2)
    for n in range(2):
        finish(n)
    factor_near(1)
    finish(2)
    finish_last(3)
    finish_last(4)
    factor_end(1, second, stores[3])
    for store in stores:
        store.wait()


def mega_call(nz, nx, *args):
    ns = nz * nx
    rows = 4 * ns
    width = 12 * ns
    half = width // 2
    vmem, sem = pltpu.VMEM, pltpu.SemaphoreType.DMA
    scratch = [
        vmem((4, rows, width), BF16),
        vmem((4, rows, rows), BF16),
        vmem((4, rows, rows), BF16),
        vmem((width, width), BF16),
        vmem((width, width), BF16),
        vmem((width, width), BF16),
        vmem((4, rows, width), BF16),
        vmem((width, 4 * rows), BF16),
        vmem((4, rows, rows), BF16),
        vmem((4, rows, rows), BF16),
    ]
    for sizes in ((1, 2, 3), (1, 2, 3), (3, 2, 1), (3, 2, 1)):
        scratch += [vmem((ns, 16, half // 3 * size), BF16) for size in sizes]
    scratch += [
        vmem((2, 4, rows, half), BF16),
        vmem((2, 4, rows, half), F32),
        vmem((2, 4, rows, half), F32),
        vmem((2, 4, rows, half), BF16),
        vmem((4, rows, half), F32),
        vmem((4, rows, half), BF16),
        vmem((2, 4, rows, half), BF16),
        vmem((2, 4, rows, half), BF16),
        vmem((2, 4, rows, half), BF16),
        vmem((half, 4 * rows), BF16),
        vmem((4, rows, width), BF16),
        vmem((4, rows, width), BF16),
        vmem((4, rows, rows), F32),
        vmem((4, rows, rows), F32),
        vmem((3, 4 * rows, half // 3), F32),
        vmem((2, width + 8, half), F32),
    ]
    for n in range(5):
        count, _ = zone_of(nz, n)
        scratch += [
            vmem((2, nx, count, 16, half), BF16),
            vmem((nx, count, 16, half), BF16),
            vmem((nx, count, 16, half), BF16),
            vmem((nx, count, 16, half), BF16),
            vmem((count, 16, half), BF16),
            vmem((4 * nz if n > 2 else 2 * nz, 16, half), BF16),
            vmem((2, 16, half), BF16),
        ]
    for _ in range(2):
        scratch += [
            vmem((2, 2, rows, rows), BF16),
            vmem((2, rows, rows), BF16),
            vmem((2, rows, rows), BF16),
            vmem((2, rows, rows), BF16),
            vmem((2, 2, rows, rows), BF16),
        ]
    scratch += [sem((count,)) for count in (12, 4, 6, 6, 20, 20, 12, 12)]
    anywhere = pl.BlockSpec(memory_space=pl.ANY)
    return pl.pallas_call(
        functools.partial(mega, nz, nx),
        out_shape=(
            jax.ShapeDtypeStruct((4, rows, width), BF16),
            jax.ShapeDtypeStruct((4, rows, width), BF16),
            jax.ShapeDtypeStruct((4, rows, rows), F32),
            jax.ShapeDtypeStruct((4, rows, rows), F32),
        )
        + (jax.ShapeDtypeStruct((12, width), F32),) * 3,
        in_specs=[anywhere] * 7,
        out_specs=(anywhere,) * 4 + (pl.BlockSpec(memory_space=vmem),) * 3,
        scratch_shapes=scratch,
        compiler_params=pltpu.CompilerParams(
            collective_id=0, has_side_effects=True, vmem_limit_bytes=60 * 2**20
        ),
        cost_estimate=pl.CostEstimate(
            flops=14 * 10**9, bytes_accessed=16 * 10**6, transcendentals=10**6
        ),
        name="mixing",
    )(*args)


def shards(
    nz, nx, tokens, first_factor, second_factor, value_weight, gate_weight, out_weight, cotangent
):
    rows, width = 4 * nz * nx, 12 * nz * nx
    result, grad, first, second, value_sum, gate_sum, out_sum = mega_call(
        nz,
        nx,
        tokens.reshape(4, rows, width),
        first_factor,
        second_factor,
        value_weight,
        gate_weight,
        out_weight,
        cotangent.reshape(4, rows, width),
    )
    return (
        result.reshape(1, 4 * rows, width),
        grad.reshape(1, 4 * rows, width),
        first,
        second,
        value_sum,
        gate_sum,
        out_sum,
    )


def solution(mesh, nz=NZ, nx=NX):
    return jax.shard_map(
        functools.partial(shards, nz, nx),
        mesh=mesh,
        in_specs=(
            P("dp", "seq", None),
            P("seq", None, None),
            P("seq", None, None),
            P(),
            P(),
            P(),
            P("dp", "seq", None),
        ),
        out_specs=(
            P("dp", "seq", None),
            P("dp", "seq", None),
            P("seq", None, None),
            P("seq", None, None),
            P("seq", None),
            P("seq", None),
            P("seq", None),
        ),
        check_vma=False,
    )
```

```python
import functools

import jax
import jax.numpy as jnp
from jax import lax
from jax.experimental import pallas as pl
from jax.experimental.pallas import tpu as pltpu
from jax.sharding import PartitionSpec as P

MESH = pl.DeviceIdType.MESH
BF16 = jnp.bfloat16
F32 = jnp.float32
NZ, NX = 4, 16


def dot(left, right):
    return jnp.dot(left, right, preferred_element_type=F32)


def dot_cols(left, right):
    return lax.dot_general(left, right, (((1,), (1,)), ((), ())), preferred_element_type=F32)


def each(count, body):
    def step(i, carry):
        body(i)
        return carry

    lax.fori_loop(0, count, step, 0)


def zone_of(nz, n):
    return ((nz, 0), (nz, 0), (nz // 2, 0), (nz // 4, nz // 2), (nz // 4, 3 * nz // 4))[n]


def mega(nz, nx, *refs):
    ns = nz * nx
    rows = 4 * ns
    width = 12 * ns
    half = width // 2
    lanes = half // 3
    side = int(nx**0.5)
    (tok_h, ff_h, sf_h, vw_h, gw_h, ow_h, cot_h), refs = refs[:7], refs[7:]
    (res, grad, first, second), w_out, refs = refs[:4], refs[4:7], refs[7:]
    (tok, ff, sf, vw, gw, ow, cot, tok_t, ff_t, sf_t), refs = refs[:10], refs[10:]
    bsend, brecv, fsend, frecv = (refs[3 * i : 3 * i + 3] for i in range(4))
    refs = refs[12:]
    (bs, val, sig, mix), refs = refs[:4], refs[4:]
    (tmp, got, dval, dgate, sec, sec_t, term, wide), refs = refs[:8], refs[8:]
    jobs = [refs[7 * n : 7 * n + 7] for n in range(5)]
    plane_b, refs = refs[35:37], refs[37:]
    facs = [refs[5 * n : 5 * n + 5] for n in range(2)]
    refs = refs[10:]
    load_sem, a2a_send, a2a_recv, job_send, job_recv, fac_send, fac_recv = refs
    a2a, job, fac = (a2a_send, a2a_recv), (job_send, job_recv), (fac_send, fac_recv)

    dp, seq = lax.axis_index("dp"), lax.axis_index("seq")
    zl, core = dp // 2, lax.rem(dp, 2)
    zh, xy = seq // nx, lax.rem(seq, nx)
    z = zh * 2 + zl
    other = 1 - core
    partner = (zl * 2 + other, seq)
    neighbour = ((1 - zl) * 2 + core, seq)

    back_groups = ((0, 0, lanes), (0, lanes, 2 * lanes), (1, 0, half))
    parts = [(sf_h, sf)]
    for c, start, size in back_groups:
        at = pl.ds(c * half + start, size)
        parts.append((ow_h.at[at, :], ow.at[at, :]))
    parts += [(cot_h.at[p], cot.at[p]) for p in range(4)]
    parts += [(tok_h, tok), (vw_h, vw), (gw_h, gw), (ff_h, ff)]
    loads = [
        pltpu.make_async_copy(src, dst, load_sem.at[i]) for i, (src, dst) in enumerate(parts)
    ]
    for i in (0, 1, 4, 5, 6, 7, 2, 3):
        loads[i].start()

    barrier = pltpu.get_barrier_semaphore()

    far = sorted(range(1, nz), key=lambda dz: abs(dz - nz / 2))

    def greet(device):
        pl.semaphore_signal(barrier, inc=1, device_id=device, device_id_type=MESH)

    def greet_row(i):
        to_xy = lax.rem(xy + i, nx)
        for dz in far:
            greet((dp, lax.rem(zh + dz, nz) * nx + to_xy))

        @pl.when(i > 0)
        def _():
            greet((dp, zh * nx + to_xy))

    def greet_column(i):
        for d in range(1, 4):
            greet((lax.rem(dp + d, 4), i * nx + xy))

    each(nx, greet_row)
    each(nz, greet_column)

    def remote(src, dst, sems, k, device):
        return pltpu.make_async_remote_copy(
            src_ref=src,
            dst_ref=dst,
            send_sem=sems[0].at[k],
            recv_sem=sems[1].at[k],
            device_id=device,
            device_id_type=MESH,
        )

    def send_all(src, dst, k):
        def send(to):
            remote(src.at[to], dst.at[seq], a2a, k, (dp, to)).start()

        def row(i):
            for dz in far:
                send(lax.rem(zh + dz, nz) * nx + lax.rem(xy + i, nx))

        each(nx, row)
        each(nx - 1, lambda i: send(zh * nx + lax.rem(xy + i + 1, nx)))
        dst[seq] = src[seq]

    def all_of(src, dst, k):
        some = pl.ds(0, ns - 1)
        return remote(src.at[some], dst.at[some], a2a, k, (dp, lax.rem(seq + 1, ns)))

    def to_messages(dst, start, size):
        tiles = min(8, rows // 8)
        mask = lax.broadcasted_iota(jnp.int32, (tiles, 8, size), 1) < 4

        def block(i):
            at = pl.ds(pl.multiple_of(i * tiles * 8, 8), tiles * 8)
            r = [tmp[k, at, start : start + size].reshape(tiles, 8, size) for k in range(4)]
            turned = [pltpu.roll(x, 4, 1) for x in r]
            low = [jnp.where(mask, r[k], turned[k + 1]) for k in (0, 2)]
            high = [jnp.where(mask, turned[k], r[k + 1]) for k in (0, 2)]
            low = jnp.concatenate(low, axis=1).astype(BF16)
            high = jnp.concatenate(high, axis=1).astype(BF16)
            for t in range(tiles):
                dst[(i * tiles + t) * 2] = low[t]
                dst[(i * tiles + t) * 2 + 1] = high[t]

        each(rows // (tiles * 8), block)

    def from_messages(src, start, size):
        for j in range(size // lanes):
            cols = slice(j * lanes, (j + 1) * lanes)
            to_cols = slice(start + j * lanes, start + (j + 1) * lanes)

            def widen(i, j=j, cols=cols):
                at = pl.ds(pl.multiple_of(i * 64, 64), 64)
                part = src[pl.ds(i * 4, 4), :, cols]
                term[j, at, :] = part.reshape(64, lanes).astype(F32)

            each(4 * rows // 64, widen)
            for k in range(4):
                got[k, :, to_cols] = term[j, pl.ds(k, rows, stride=4), :].astype(BF16)

    def zone(n):
        count, base = zone_of(nz, n)
        inside = (zh >= base) & (zh < base + count)
        return count, base, inside, inside & (zl == n % 2)

    def put_rows(n, which, start, stop, offset=0):
        own = jobs[n][0]

        def two(i):
            m = start + i
            x = wide[which, pl.ds(pl.multiple_of(24 * (m + offset), 8), 32), :]
            for k in range(2):
                s = 2 * m + k
                block = x[12 * k : 12 * k + 16].astype(BF16)
                place = lax.rem(s, nx)
                if n < 2 and which == 1:
                    place = lax.rem(place, side) * side + place // side
                own[which, place, s // nx] = block

        each(stop - start, two)

    def pair_copy(n):
        return remote(jobs[n][0].at[other], jobs[n][1], job, 5 * n, partner)

    def pair_add(n):
        own, pair, u, plane = jobs[n][:4]
        pair_copy(n).wait()

        def add(i):
            u[i] = (own[core, i].astype(F32) + pair[i].astype(F32)).astype(BF16)

        each(nx, add)
        if n < 2:

            def send_side(i):
                to = lax.rem(mine + i + 1, side)
                src, dst = u.at[pl.ds(to * side, side)], plane.at[pl.ds(mine * side, side)]
                remote(src, dst, job, 5 * n + 1, along(to, crossed)).start()

            each(side - 1, send_side)

            def keep(i):
                plane[mine * side + i] = u[mine * side + i]

            each(side, keep)
        else:

            def send(i):
                to = lax.rem(xy + i + 1, nx)
                remote(u.at[to], plane.at[xy], job, 5 * n + 1, (dp, zh * nx + to)).start()

            each(nx - 1, send)
            plane[xy] = u[xy]

    mine = (1 - core) * (xy // side) + core * lax.rem(xy, side)
    crossed = core * (xy // side) + (1 - core) * lax.rem(xy, side)

    def along(at_mine, at_crossed):
        place = (1 - core) * (at_mine * side + at_crossed) + core * (at_crossed * side + at_mine)
        return dp, zh * nx + place

    def side_add(n):
        u, plane = jobs[n][2:4]
        some = pl.ds(0, (side - 1) * side)
        remote(u.at[some], plane.at[some], job, 5 * n + 1, partner).wait()

        def add(i):
            x = plane[i].astype(F32)
            for k in range(1, side):
                x = x + plane[k * side + i].astype(F32)
            u[i] = x.astype(BF16)

        each(side, add)

        def send(i):
            to = lax.rem(crossed + i + 1, side)
            remote(
                u.at[to], plane_b[n].at[crossed], job, 5 * n + 4, along(mine, to)
            ).start()

        each(side - 1, send)
        plane_b[n][crossed] = u[crossed]

    def plane_add(n):
        u, plane, total, col = jobs[n][2:6]
        count, base, inside, member = zone(n)
        if n < 2:
            some = pl.ds(0, side - 1)
            plane, sources = plane_b[n], side
            remote(u.at[some], plane.at[some], job, 5 * n + 4, partner).wait()
        else:
            some, sources = pl.ds(0, nx - 1), nx
            remote(u.at[some], plane.at[some], job, 5 * n + 1, partner).wait()

        def add(q):
            x = plane[0, q].astype(F32)
            for i in range(1, sources):
                x = x + plane[i, q].astype(F32)
            total[q] = x.astype(BF16)

        each(count, add)
        if n < 3:

            def send(i):
                @pl.when((base + i != zh) | (zl != n % 2))
                def _():
                    device = ((n % 2) * 2 + core, (base + i) * nx + xy)
                    remote(total.at[i], col.at[z], job, 5 * n + 2, device).start()

            each(count, send)

            @pl.when(member)
            def _():
                col[z] = total[zh - base]

        else:

            def send(i):
                to_dp = lax.rem(i, 4)

                @pl.when((base + i // 4 != zh) | (to_dp != dp))
                def _():
                    device = (to_dp, (base + i // 4) * nx + xy)
                    slot = col.at[core * 2 * nz + z]
                    remote(total.at[i // 4], slot, job, 5 * n + 2, device).start()

            each(4 * count, send)

            @pl.when(inside)
            def _():
                col[core * 2 * nz + z] = total[zh - base]

    def pieces(n, sem, size):
        some = pl.ds(0, size)
        return remote(jobs[n][5].at[some], jobs[n][5].at[some], job, 5 * n + sem, partner)

    def sum_of(col, start):
        x = col[start].astype(F32)
        for i in range(1, 2 * nz):
            x = x + col[start + i].astype(F32)
        return x

    def column_add(n):
        col, fin = jobs[n][5:]
        count, _, _, member = zone(n)

        @pl.when(member)
        def _():
            pieces(n, 2, 2 * nz - 1).wait_recv()
            fin[core] = sum_of(col, 0).astype(BF16)
            for d in range(1, 4):
                device = (lax.rem(dp + d, 4), seq)
                remote(fin.at[core], fin.at[core], job, 5 * n + 3, device).start()
            pieces(n, 2, count - 1).wait_send()

        @pl.when(jnp.logical_not(member))
        def _():
            pieces(n, 2, count).wait_send()

    def finish(n):
        fin = jobs[n][6]
        _, _, inside, member = zone(n)

        @pl.when(inside)
        def _():
            @pl.when(member)
            def _():
                remote(fin.at[other], fin.at[other], job, 5 * n + 3, partner).wait_recv()
                pieces(n, 3, 3).wait_send()

            @pl.when(jnp.logical_not(member))
            def _():
                remote(fin, fin, job, 5 * n + 3, partner).wait_recv()

            at = [
                ((0, slice(0, half)), (1, slice(0, half))),
                ((0, slice(half, width)), (1, slice(half, width))),
                ((2, slice(0, half)), (2, slice(half, width))),
            ][n]
            for k in range(2):
                w_out[at[k][0]][:, at[k][1]] = fin[k].astype(F32)[:12]

    def finish_last(n):
        col = jobs[n][5]
        count, _, inside, _ = zone(n)

        @pl.when(inside)
        def _():
            pieces(n, 2, 4 * nz - 1).wait_recv()
            for k in range(2):
                total = sum_of(col, 2 * nz * k).astype(BF16)
                w_out[2][:, k * half : (k + 1) * half] = total.astype(F32)[:12]
            pieces(n, 2, 4 * count - 1).wait_send()

        @pl.when(jnp.logical_not(inside))
        def _():
            pieces(n, 2, 4 * count).wait_send()

    def factor_copy(n, k):
        own, pair = facs[n][:2]
        return remote(own.at[other, k], pair.at[k], fac, 6 * n + k, partner)

    def factor_start(n, source):
        own = facs[n][0]
        for k in range(2):
            for h in range(2):
                own[h, k] = source[2 * h + k].astype(BF16)
            factor_copy(n, k).start()

    def factor_pair(n, send):
        own, pair, u = facs[n][:3]
        for k in range(2):
            factor_copy(n, k).wait()
            u[k] = (own[core, k].astype(F32) + pair[k].astype(F32)).astype(BF16)
            if k < send:
                near_copy(n, k).start()

    def near_copy(n, k):
        return remote(facs[n][2].at[k], facs[n][3].at[k], fac, 6 * n + 2 + k, neighbour)

    def fin_copy(n, k):
        fin = facs[n][4]
        return remote(fin.at[core, k], fin.at[core, k], fac, 6 * n + 4 + k, partner)

    def factor_near(n):
        _, _, u, near, fin = facs[n]
        for k in range(2):
            near_copy(n, k).wait()
            fin[core, k] = (u[k].astype(F32) + near[k].astype(F32)).astype(BF16)
            fin_copy(n, k).start()

    def factor_end(n, wide_sum):
        fin = facs[n][4]
        for k in range(2):
            fin_copy(n, k).wait()
        for k in range(4):
            wide_sum[k] = fin[k // 2, k % 2].astype(F32)

    for which in range(2):
        wide[which, width:, :] = jnp.zeros((8, half), F32)

    for g, (c, start, size) in enumerate(back_groups):
        loads[1 + g].wait()

        def back(p, c=c, start=start, size=size):
            at = c * half + start
            part = dot_cols(cot[p], ow[at : at + size, :]).astype(BF16)
            bs[c, p, :, start : start + size] = part
            tmp[p, :, :size] = dot(sf_t[p], part)

        if g == 0:
            loads[0].wait()
            for p in range(4):
                sf_t[p] = sf[p].T
                loads[4 + p].wait()
                back(p)
            for load in loads[8:]:
                load.start()
        else:
            each(4, back)
        to_messages(bsend[g], 0, size)
        if g == 0:
            pl.semaphore_wait(barrier, ns - 1 + 3 * nz)
        send_all(bsend[g], brecv[g], g)

    for load in loads[8:]:
        load.wait()
    forward_groups = ((0, 0, half), (1, 0, 2 * lanes), (1, 2 * lanes, lanes))
    for c in range(2):
        cols = slice(c * half, (c + 1) * half)

        def forward(a, c=c, cols=cols):
            v = dot(tok[a], vw[:, cols])
            s = jax.nn.sigmoid(dot(tok[a], gw[:, cols]))
            m = (v * s).astype(BF16)
            val[c, a] = v
            sig[c, a] = s
            mix[c, a] = m
            tmp[a] = dot(ff[a], m)

        each(4, forward)
        for g, (group_c, start, size) in enumerate(forward_groups):
            if group_c == c:
                to_messages(fsend[g], start, size)
    for k in range(4):
        ff_t[k] = ff[k].T
        tok_t[:, k * rows : (k + 1) * rows] = tok[k].T

    def back_copy(g):
        return all_of(bsend[g], brecv[g], g)

    def forward_copy(g):
        return all_of(fsend[g], frecv[g], 3 + g)

    for c in range(2):
        groups = [g for g in range(3) if back_groups[g][0] == c]
        for g in groups:
            back_copy(g).wait_send()
        for g in range(3):
            if forward_groups[g][0] == c:
                send_all(fsend[g], frecv[g], 3 + g)
        if c == 1:
            pair_add(0)
        for g in groups:
            back_copy(g).wait_recv()
            from_messages(brecv[g], *back_groups[g][1:])

        def inner(a, c=c):
            g = got[a]
            part = dot(ff_t[a], g)
            s = sig[c, a]
            ps = part * s
            dval[c, a] = ps.astype(BF16)
            dgate[c, a] = (ps * val[c, a] * (1.0 - s)).astype(BF16)
            more = dot_cols(g, mix[c, a])
            if c == 0:
                first[a] = more
            else:
                first[a] = first[a] + more

        each(4, inner)
        for which, source in enumerate((dval, dgate)):

            def terms(m, c=c, which=which, source=source):
                at = pl.ds(pl.multiple_of(m * rows, 8), rows)
                wide[which, at, :] = dot(tok_t[at, :], source[c].reshape(4 * rows, half))

            each(3, terms)
            put_rows(c, which, 0, ns // 2)
        pair_copy(c).start()
    factor_start(0, first)
    side_add(0)
    pair_add(1)
    factor_pair(0, 1)

    def grads(a):
        x = dot_cols(dval[0, a], vw[:, :half]) + dot_cols(dval[1, a], vw[:, half:])
        y = dot_cols(dgate[0, a], gw[:, :half]) + dot_cols(dgate[1, a], gw[:, half:])
        grad[a] = (x + y).astype(BF16)

    each(4, grads)
    plane_add(0)
    side_add(1)

    def mix_second(g):
        c, start, size = forward_groups[g]
        cols = slice(start, start + size)
        forward_copy(g).wait_recv()
        from_messages(frecv[g], start, size)

        def inner(p):
            sec[c, p, :, cols] = dot(sf[p], got[p, :, cols]).astype(BF16)

        each(4, inner)
        for k in range(4):
            sec_t[cols, k * rows : (k + 1) * rows] = sec[c, k, :, cols].T
        for which in range(2):
            right = cot[:, :, which * half : (which + 1) * half].reshape(4 * rows, half)
            wide[which, cols, :] = dot(sec_t[cols, :], right)

    def grow_second(g):
        c, start, size = forward_groups[g]
        cols = slice(start, start + size)

        def outer(p):
            more = dot_cols(bs[c, p, :, cols], got[p, :, cols])
            if g == 0:
                second[p] = more
            else:
                second[p] = second[p] + more

        each(4, outer)

    mix_second(0)
    for which in range(2):
        put_rows(2, which, 0, ns // 4)
    pair_copy(2).start()
    grow_second(0)
    plane_add(1)
    pair_add(2)
    pairs = ns // 8
    early = 2 * lanes // 24 - pairs
    mix_second(1)
    for which in range(2):
        put_rows(3, which, 0, pairs)
    pair_copy(3).start()
    for which in range(2):
        put_rows(4, which, 0, early, pairs)
    grow_second(1)
    pair_add(3)
    for g in range(3):
        forward_copy(g).wait_send()
    near_copy(0, 1).start()
    plane_add(2)
    column_add(0)
    column_add(1)
    mix_second(2)
    for which in range(2):
        put_rows(4, which, early, pairs, pairs)
    pair_copy(4).start()
    grow_second(2)
    factor_start(1, second)
    pair_add(4)
    factor_pair(1, 2)
    plane_add(3)
    factor_near(0)

    def results(p):
        x = dot(sec[0, p], ow[:half, :]) + dot(sec[1, p], ow[half:, :])
        res[p] = x.astype(BF16)

    each(4, results)
    factor_end(0, first)
    plane_add(4)
    column_add(2)
    for n in range(2):
        finish(n)
    factor_near(1)
    finish(2)
    finish_last(3)
    finish_last(4)
    factor_end(1, second)


def mega_call(nz, nx, *args):
    ns = nz * nx
    rows = 4 * ns
    width = 12 * ns
    half = width // 2
    vmem, sem = pltpu.VMEM, pltpu.SemaphoreType.DMA
    scratch = [
        vmem((4, rows, width), BF16),
        vmem((4, rows, rows), BF16),
        vmem((4, rows, rows), BF16),
        vmem((width, width), BF16),
        vmem((width, width), BF16),
        vmem((width, width), BF16),
        vmem((4, rows, width), BF16),
        vmem((width, 4 * rows), BF16),
        vmem((4, rows, rows), BF16),
        vmem((4, rows, rows), BF16),
    ]
    for sizes in ((1, 2, 3), (1, 2, 3), (3, 2, 1), (3, 2, 1)):
        scratch += [vmem((ns, 16, half // 3 * size), BF16) for size in sizes]
    scratch += [
        vmem((2, 4, rows, half), BF16),
        vmem((2, 4, rows, half), F32),
        vmem((2, 4, rows, half), F32),
        vmem((2, 4, rows, half), BF16),
        vmem((4, rows, half), F32),
        vmem((4, rows, half), BF16),
        vmem((2, 4, rows, half), BF16),
        vmem((2, 4, rows, half), BF16),
        vmem((2, 4, rows, half), BF16),
        vmem((half, 4 * rows), BF16),
        vmem((3, 4 * rows, half // 3), F32),
        vmem((2, width + 8, half), F32),
    ]
    for n in range(5):
        count, _ = zone_of(nz, n)
        scratch += [
            vmem((2, nx, count, 16, half), BF16),
            vmem((nx, count, 16, half), BF16),
            vmem((nx, count, 16, half), BF16),
            vmem((nx, count, 16, half), BF16),
            vmem((count, 16, half), BF16),
            vmem((4 * nz if n > 2 else 2 * nz, 16, half), BF16),
            vmem((2, 16, half), BF16),
        ]
    scratch += [vmem((int(nx**0.5), nz, 16, half), BF16)] * 2
    for _ in range(2):
        scratch += [
            vmem((2, 2, rows, rows), BF16),
            vmem((2, rows, rows), BF16),
            vmem((2, rows, rows), BF16),
            vmem((2, rows, rows), BF16),
            vmem((2, 2, rows, rows), BF16),
        ]
    scratch += [sem((count,)) for count in (12, 6, 6, 25, 25, 12, 12)]
    anywhere = pl.BlockSpec(memory_space=pl.ANY)
    return pl.pallas_call(
        functools.partial(mega, nz, nx),
        out_shape=(vmem((4, rows, width), BF16),) * 2
        + (vmem((4, rows, rows), F32),) * 2
        + (vmem((12, width), F32),) * 3,
        in_specs=[anywhere] * 7,
        out_specs=(pl.BlockSpec(memory_space=vmem),) * 7,
        scratch_shapes=scratch,
        compiler_params=pltpu.CompilerParams(
            collective_id=0, has_side_effects=True, vmem_limit_bytes=53 * 2**20
        ),
        cost_estimate=pl.CostEstimate(
            flops=14 * 10**9, bytes_accessed=16 * 10**6, transcendentals=10**6
        ),
        name="mixing",
    )(*args)


def deliver(*refs):
    sources, targets, sem = refs[:7], refs[7:14], refs[14]
    copies = []
    for src, dst in zip(sources, targets):
        for i in range(src.shape[0] if len(src.shape) == 3 else 1):
            pair = (src.at[i], dst.at[i]) if len(src.shape) == 3 else (src, dst)
            copies.append(pltpu.make_async_copy(*pair, sem.at[len(copies)]))
    for copy in copies:
        copy.start()
    for copy in copies:
        copy.wait()


def deliver_call(arrays):
    return pl.pallas_call(
        deliver,
        out_shape=tuple(jax.ShapeDtypeStruct(x.shape, x.dtype) for x in arrays),
        in_specs=[pl.BlockSpec(memory_space=pltpu.VMEM)] * 7,
        out_specs=(pl.BlockSpec(memory_space=pl.ANY),) * 7,
        scratch_shapes=[pltpu.SemaphoreType.DMA((19,))],
        compiler_params=pltpu.CompilerParams(vmem_limit_bytes=2**20),
        name="deliver",
    )(*arrays)


def shards(
    nz, nx, tokens, first_factor, second_factor, value_weight, gate_weight, out_weight, cotangent
):
    rows, width = 4 * nz * nx, 12 * nz * nx
    arrays = mega_call(
        nz,
        nx,
        tokens.reshape(4, rows, width),
        first_factor,
        second_factor,
        value_weight,
        gate_weight,
        out_weight,
        cotangent.reshape(4, rows, width),
    )
    result, grad, first, second, value_sum, gate_sum, out_sum = deliver_call(arrays)
    return (
        result.reshape(1, 4 * rows, width),
        grad.reshape(1, 4 * rows, width),
        first,
        second,
        value_sum,
        gate_sum,
        out_sum,
    )


def solution(mesh, nz=NZ, nx=NX):
    return jax.shard_map(
        functools.partial(shards, nz, nx),
        mesh=mesh,
        in_specs=(
            P("dp", "seq", None),
            P("seq", None, None),
            P("seq", None, None),
            P(),
            P(),
            P(),
            P("dp", "seq", None),
        ),
        out_specs=(
            P("dp", "seq", None),
            P("dp", "seq", None),
            P("seq", None, None),
            P("seq", None, None),
            P("seq", None),
            P("seq", None),
            P("seq", None),
        ),
        check_vma=False,
    )
```

```python
import functools

import jax
import jax.numpy as jnp
from jax import lax
from jax.experimental import pallas as pl
from jax.experimental.pallas import tpu as pltpu
from jax.sharding import PartitionSpec as P

MESH = pl.DeviceIdType.MESH
BF16 = jnp.bfloat16
F32 = jnp.float32
NZ, NX = 4, 16


def dot(left, right):
    return jnp.dot(left, right, preferred_element_type=F32)


def dot_cols(left, right):
    return lax.dot_general(left, right, (((1,), (1,)), ((), ())), preferred_element_type=F32)


def each(count, body):
    def step(i, carry):
        body(i)
        return carry

    lax.fori_loop(0, count, step, 0)


def zone_of(nz, n):
    return ((nz, 0), (nz, 0), (nz // 2, 0), (nz // 4, nz // 2), (nz // 4, 3 * nz // 4))[n]


def mega(nz, nx, *refs):
    ns = nz * nx
    rows = 4 * ns
    width = 12 * ns
    half = width // 2
    lanes = half // 3
    side = int(nx**0.5)
    (tok_h, ff_h, sf_h, vw_h, gw_h, ow_h, cot_h), refs = refs[:7], refs[7:]
    (res, grad, first, second), w_out, refs = refs[:4], refs[4:7], refs[7:]
    (tok, ff, sf, vw, gw, ow, cot, tok_t, ff_t, sf_t), refs = refs[:10], refs[10:]
    bsend, brecv, fsend, frecv = (refs[3 * i : 3 * i + 3] for i in range(4))
    refs = refs[12:]
    (bs, val, sig, mix), refs = refs[:4], refs[4:]
    (tmp, got, dval, dgate, sec, sec_t, term, wide), refs = refs[:8], refs[8:]
    jobs = [refs[7 * n : 7 * n + 7] for n in range(5)]
    plane_b, refs = refs[35:37], refs[37:]
    facs = [refs[5 * n : 5 * n + 5] for n in range(2)]
    refs = refs[10:]
    load_sem, a2a_send, a2a_recv, job_send, job_recv, fac_send, fac_recv = refs
    a2a, job, fac = (a2a_send, a2a_recv), (job_send, job_recv), (fac_send, fac_recv)

    dp, seq = lax.axis_index("dp"), lax.axis_index("seq")
    zl, core = dp // 2, lax.rem(dp, 2)
    zh, xy = seq // nx, lax.rem(seq, nx)
    z = zh * 2 + zl
    other = 1 - core
    partner = (zl * 2 + other, seq)
    neighbour = ((1 - zl) * 2 + core, seq)

    back_groups = ((0, 0, lanes), (0, lanes, 2 * lanes), (1, 0, half))
    parts = [(sf_h, sf)]
    for c, start, size in back_groups:
        at = pl.ds(c * half + start, size)
        parts.append((ow_h.at[at, :], ow.at[at, :]))
    parts += [(cot_h.at[p], cot.at[p]) for p in range(4)]
    parts += [(tok_h, tok), (vw_h, vw), (gw_h, gw), (ff_h, ff)]
    loads = [
        pltpu.make_async_copy(src, dst, load_sem.at[i]) for i, (src, dst) in enumerate(parts)
    ]
    for i in (0, 1, 4, 5, 6, 7, 2, 3):
        loads[i].start()

    barrier = pltpu.get_barrier_semaphore()

    far = sorted(range(1, nz), key=lambda dz: abs(dz - nz / 2))

    def greet(device):
        pl.semaphore_signal(barrier, inc=1, device_id=device, device_id_type=MESH)

    def greet_row(i):
        to_xy = lax.rem(xy + i, nx)
        for dz in far:
            greet((dp, lax.rem(zh + dz, nz) * nx + to_xy))

        @pl.when(i > 0)
        def _():
            greet((dp, zh * nx + to_xy))

    def greet_column(i):
        for d in range(1, 4):
            greet((lax.rem(dp + d, 4), i * nx + xy))

    each(nx, greet_row)
    each(nz, greet_column)

    def remote(src, dst, sems, k, device):
        return pltpu.make_async_remote_copy(
            src_ref=src,
            dst_ref=dst,
            send_sem=sems[0].at[k],
            recv_sem=sems[1].at[k],
            device_id=device,
            device_id_type=MESH,
        )

    def send_all(src, dst, k):
        def send(to):
            remote(src.at[to], dst.at[seq], a2a, k, (dp, to)).start()

        def row(i):
            for dz in far:
                send(lax.rem(zh + dz, nz) * nx + lax.rem(xy + i, nx))

        each(nx, row)
        each(nx - 1, lambda i: send(zh * nx + lax.rem(xy + i + 1, nx)))
        dst[seq] = src[seq]

    def all_of(src, dst, k):
        some = pl.ds(0, ns - 1)
        return remote(src.at[some], dst.at[some], a2a, k, (dp, lax.rem(seq + 1, ns)))

    def to_messages(dst, start, size):
        tiles = min(8, rows // 8)
        mask = lax.broadcasted_iota(jnp.int32, (tiles, 8, size), 1) < 4

        def block(i):
            at = pl.ds(pl.multiple_of(i * tiles * 8, 8), tiles * 8)
            r = [tmp[k, at, start : start + size].reshape(tiles, 8, size) for k in range(4)]
            turned = [pltpu.roll(x, 4, 1) for x in r]
            low = [jnp.where(mask, r[k], turned[k + 1]) for k in (0, 2)]
            high = [jnp.where(mask, turned[k], r[k + 1]) for k in (0, 2)]
            low = jnp.concatenate(low, axis=1).astype(BF16)
            high = jnp.concatenate(high, axis=1).astype(BF16)
            for t in range(tiles):
                dst[(i * tiles + t) * 2] = low[t]
                dst[(i * tiles + t) * 2 + 1] = high[t]

        each(rows // (tiles * 8), block)

    def from_messages(src, start, size):
        for j in range(size // lanes):
            cols = slice(j * lanes, (j + 1) * lanes)
            to_cols = slice(start + j * lanes, start + (j + 1) * lanes)

            def widen(i, j=j, cols=cols):
                at = pl.ds(pl.multiple_of(i * 64, 64), 64)
                part = src[pl.ds(i * 4, 4), :, cols]
                term[j, at, :] = part.reshape(64, lanes).astype(F32)

            each(4 * rows // 64, widen)
            for k in range(4):
                got[k, :, to_cols] = term[j, pl.ds(k, rows, stride=4), :].astype(BF16)

    def zone(n):
        count, base = zone_of(nz, n)
        inside = (zh >= base) & (zh < base + count)
        return count, base, inside, inside & (zl == n % 2)

    def put_rows(n, which, start, stop, offset=0):
        own = jobs[n][0]

        def two(i):
            m = start + i
            x = wide[which, pl.ds(pl.multiple_of(24 * (m + offset), 8), 32), :]
            for k in range(2):
                s = 2 * m + k
                block = x[12 * k : 12 * k + 16].astype(BF16)
                place = lax.rem(s, nx)
                if n < 2 and which == 1:
                    place = lax.rem(place, side) * side + place // side
                own[which, place, s // nx] = block

        each(stop - start, two)

    def pair_copy(n):
        return remote(jobs[n][0].at[other], jobs[n][1], job, 5 * n, partner)

    def pair_add(n):
        own, pair, u, plane = jobs[n][:4]
        pair_copy(n).wait()

        def add(i):
            u[i] = (own[core, i].astype(F32) + pair[i].astype(F32)).astype(BF16)

        each(nx, add)
        if n < 2:

            def send_side(i):
                to = lax.rem(mine + i + 1, side)
                src, dst = u.at[pl.ds(to * side, side)], plane.at[pl.ds(mine * side, side)]
                remote(src, dst, job, 5 * n + 1, along(to, crossed)).start()

            each(side - 1, send_side)

            def keep(i):
                plane[mine * side + i] = u[mine * side + i]

            each(side, keep)
        else:

            def send(i):
                to = lax.rem(xy + i + 1, nx)
                remote(u.at[to], plane.at[xy], job, 5 * n + 1, (dp, zh * nx + to)).start()

            each(nx - 1, send)
            plane[xy] = u[xy]

    mine = (1 - core) * (xy // side) + core * lax.rem(xy, side)
    crossed = core * (xy // side) + (1 - core) * lax.rem(xy, side)

    def along(at_mine, at_crossed):
        place = (1 - core) * (at_mine * side + at_crossed) + core * (at_crossed * side + at_mine)
        return dp, zh * nx + place

    def side_add(n):
        u, plane = jobs[n][2:4]
        some = pl.ds(0, (side - 1) * side)
        remote(u.at[some], plane.at[some], job, 5 * n + 1, partner).wait()

        def add(i):
            x = plane[i].astype(F32)
            for k in range(1, side):
                x = x + plane[k * side + i].astype(F32)
            u[i] = x.astype(BF16)

        each(side, add)

        def send(i):
            to = lax.rem(crossed + i + 1, side)
            remote(
                u.at[to], plane_b[n].at[crossed], job, 5 * n + 4, along(mine, to)
            ).start()

        each(side - 1, send)
        plane_b[n][crossed] = u[crossed]

    def plane_add(n):
        u, plane, total, col = jobs[n][2:6]
        count, base, inside, member = zone(n)
        if n < 2:
            some = pl.ds(0, side - 1)
            plane, sources = plane_b[n], side
            remote(u.at[some], plane.at[some], job, 5 * n + 4, partner).wait()
        else:
            some, sources = pl.ds(0, nx - 1), nx
            remote(u.at[some], plane.at[some], job, 5 * n + 1, partner).wait()

        def add(q):
            x = plane[0, q].astype(F32)
            for i in range(1, sources):
                x = x + plane[i, q].astype(F32)
            total[q] = x.astype(BF16)

        each(count, add)
        if n < 3:

            def send(i):
                @pl.when((base + i != zh) | (zl != n % 2))
                def _():
                    device = ((n % 2) * 2 + core, (base + i) * nx + xy)
                    remote(total.at[i], col.at[z], job, 5 * n + 2, device).start()

            each(count, send)

            @pl.when(member)
            def _():
                col[z] = total[zh - base]

        else:

            def send(i):
                to_dp = lax.rem(i, 4)

                @pl.when((base + i // 4 != zh) | (to_dp != dp))
                def _():
                    device = (to_dp, (base + i // 4) * nx + xy)
                    slot = col.at[core * 2 * nz + z]
                    remote(total.at[i // 4], slot, job, 5 * n + 2, device).start()

            each(4 * count, send)

            @pl.when(inside)
            def _():
                col[core * 2 * nz + z] = total[zh - base]

    def pieces(n, sem, size):
        some = pl.ds(0, size)
        return remote(jobs[n][5].at[some], jobs[n][5].at[some], job, 5 * n + sem, partner)

    def sum_of(col, start):
        x = col[start].astype(F32)
        for i in range(1, 2 * nz):
            x = x + col[start + i].astype(F32)
        return x

    def column_add(n):
        col, fin = jobs[n][5:]
        count, _, _, member = zone(n)

        @pl.when(member)
        def _():
            pieces(n, 2, 2 * nz - 1).wait_recv()
            fin[core] = sum_of(col, 0).astype(BF16)
            for d in range(1, 4):
                device = (lax.rem(dp + d, 4), seq)
                remote(fin.at[core], fin.at[core], job, 5 * n + 3, device).start()
            pieces(n, 2, count - 1).wait_send()

        @pl.when(jnp.logical_not(member))
        def _():
            pieces(n, 2, count).wait_send()

    def finish(n):
        fin = jobs[n][6]
        _, _, inside, member = zone(n)

        @pl.when(inside)
        def _():
            @pl.when(member)
            def _():
                remote(fin.at[other], fin.at[other], job, 5 * n + 3, partner).wait_recv()
                pieces(n, 3, 3).wait_send()

            @pl.when(jnp.logical_not(member))
            def _():
                remote(fin, fin, job, 5 * n + 3, partner).wait_recv()

            at = [
                ((0, slice(0, half)), (1, slice(0, half))),
                ((0, slice(half, width)), (1, slice(half, width))),
                ((2, slice(0, half)), (2, slice(half, width))),
            ][n]
            for k in range(2):
                w_out[at[k][0]][:, at[k][1]] = fin[k].astype(F32)[:12]

    def finish_last(n):
        col = jobs[n][5]
        count, _, inside, _ = zone(n)

        @pl.when(inside)
        def _():
            pieces(n, 2, 4 * nz - 1).wait_recv()
            for k in range(2):
                total = sum_of(col, 2 * nz * k).astype(BF16)
                w_out[2][:, k * half : (k + 1) * half] = total.astype(F32)[:12]
            pieces(n, 2, 4 * count - 1).wait_send()

        @pl.when(jnp.logical_not(inside))
        def _():
            pieces(n, 2, 4 * count).wait_send()

    def factor_copy(n, k):
        own, pair = facs[n][:2]
        return remote(own.at[other, k], pair.at[k], fac, 6 * n + k, partner)

    def factor_start(n, source, before=None):
        own = facs[n][0]
        for k in range(2):
            for h in range(2):
                if before is not None:
                    before(2 * h + k)
                own[h, k] = source[2 * h + k].astype(BF16)
            factor_copy(n, k).start()

    def factor_pair(n, send):
        own, pair, u = facs[n][:3]
        for k in range(2):
            factor_copy(n, k).wait()
            u[k] = (own[core, k].astype(F32) + pair[k].astype(F32)).astype(BF16)
            if k < send:
                near_copy(n, k).start()

    def near_copy(n, k):
        return remote(facs[n][2].at[k], facs[n][3].at[k], fac, 6 * n + 2 + k, neighbour)

    def fin_copy(n, k):
        fin = facs[n][4]
        return remote(fin.at[core, k], fin.at[core, k], fac, 6 * n + 4 + k, partner)

    def factor_near(n):
        _, _, u, near, fin = facs[n]
        for k in range(2):
            near_copy(n, k).wait()
            fin[core, k] = (u[k].astype(F32) + near[k].astype(F32)).astype(BF16)
            fin_copy(n, k).start()

    def factor_end(n, wide_sum):
        fin = facs[n][4]
        for k in range(2):
            fin_copy(n, k).wait()
        for k in range(4):
            wide_sum[k] = fin[k // 2, k % 2].astype(F32)

    for which in range(2):
        wide[which, width:, :] = jnp.zeros((8, half), F32)

    for g, (c, start, size) in enumerate(back_groups):
        loads[1 + g].wait()

        def back(p, c=c, start=start, size=size):
            at = c * half + start
            part = dot_cols(cot[p], ow[at : at + size, :]).astype(BF16)
            bs[c, p, :, start : start + size] = part
            tmp[p, :, :size] = dot(sf_t[p], part)

        if g == 0:
            loads[0].wait()
            for p in range(4):
                sf_t[p] = sf[p].T
                loads[4 + p].wait()
                back(p)
            for load in loads[8:]:
                load.start()
        else:
            each(4, back)
        to_messages(bsend[g], 0, size)
        if g == 0:
            pl.semaphore_wait(barrier, ns - 1 + 3 * nz)
        send_all(bsend[g], brecv[g], g)

    for load in loads[8:]:
        load.wait()
    forward_groups = ((0, 0, half), (1, 0, 2 * lanes), (1, 2 * lanes, lanes))
    for c in range(2):
        cols = slice(c * half, (c + 1) * half)

        def forward(a, c=c, cols=cols):
            v = dot(tok[a], vw[:, cols])
            s = jax.nn.sigmoid(dot(tok[a], gw[:, cols]))
            m = (v * s).astype(BF16)
            val[c, a] = v
            sig[c, a] = s
            mix[c, a] = m
            tmp[a] = dot(ff[a], m)

        each(4, forward)
        for g, (group_c, start, size) in enumerate(forward_groups):
            if group_c == c:
                to_messages(fsend[g], start, size)
    for k in range(4):
        ff_t[k] = ff[k].T
        tok_t[:, k * rows : (k + 1) * rows] = tok[k].T

    def back_copy(g):
        return all_of(bsend[g], brecv[g], g)

    def forward_copy(g):
        return all_of(fsend[g], frecv[g], 3 + g)

    for c in range(2):
        groups = [g for g in range(3) if back_groups[g][0] == c]
        if c == 1:
            pair_add(0)
        for g in groups:
            back_copy(g).wait_send()
        for g in range(3):
            if forward_groups[g][0] == c:
                send_all(fsend[g], frecv[g], 3 + g)
        for g in groups:
            back_copy(g).wait_recv()
            from_messages(brecv[g], *back_groups[g][1:])

        def inner(a, c=c):
            g = got[a]
            part = dot(ff_t[a], g)
            s = sig[c, a]
            ps = part * s
            dval[c, a] = ps.astype(BF16)
            dgate[c, a] = (ps * val[c, a] * (1.0 - s)).astype(BF16)
            more = dot_cols(g, mix[c, a])
            if c == 0:
                first[a] = more
            else:
                first[a] = first[a] + more

        each(4, inner)
        for which, source in enumerate((dval, dgate)):

            def terms(m, c=c, which=which, source=source):
                at = pl.ds(pl.multiple_of(m * rows, 8), rows)
                wide[which, at, :] = dot(tok_t[at, :], source[c].reshape(4 * rows, half))

            each(3, terms)
            put_rows(c, which, 0, ns // 2)
        pair_copy(c).start()
    factor_start(0, first)
    side_add(0)
    pair_add(1)
    factor_pair(0, 1)

    def grads(a):
        x = dot_cols(dval[0, a], vw[:, :half]) + dot_cols(dval[1, a], vw[:, half:])
        y = dot_cols(dgate[0, a], gw[:, :half]) + dot_cols(dgate[1, a], gw[:, half:])
        grad[a] = (x + y).astype(BF16)

    each(4, grads)
    plane_add(0)
    side_add(1)

    def take(g):
        forward_copy(g).wait_recv()
        from_messages(frecv[g], *forward_groups[g][1:])

    def mix_second(g):
        c, start, size = forward_groups[g]
        cols = slice(start, start + size)
        def inner(p):
            sec[c, p, :, cols] = dot(sf[p], got[p, :, cols]).astype(BF16)

        each(4, inner)
        for k in range(4):
            sec_t[cols, k * rows : (k + 1) * rows] = sec[c, k, :, cols].T
        for which in range(2):
            right = cot[:, :, which * half : (which + 1) * half].reshape(4 * rows, half)
            wide[which, cols, :] = dot(sec_t[cols, :], right)

    def grow(g, p):
        c, start, size = forward_groups[g]
        cols = slice(start, start + size)
        more = dot_cols(bs[c, p, :, cols], got[p, :, cols])
        if g == 0:
            second[p] = more
        else:
            second[p] = second[p] + more

    def grow_second(g):
        each(4, functools.partial(grow, g))

    take(0)
    mix_second(0)
    for which in range(2):
        put_rows(2, which, 0, ns // 4)
    pair_copy(2).start()
    grow_second(0)
    plane_add(1)
    pair_add(2)
    pairs = ns // 8
    early = 2 * lanes // 24 - pairs
    take(1)
    mix_second(1)
    for which in range(2):
        put_rows(3, which, 0, pairs)
    pair_copy(3).start()
    for which in range(2):
        put_rows(4, which, 0, early, pairs)
    grow_second(1)
    pair_add(3)
    for g in range(3):
        forward_copy(g).wait_send()
    near_copy(0, 1).start()
    plane_add(2)
    column_add(0)
    column_add(1)
    take(2)
    factor_start(1, second, functools.partial(grow, 2))
    mix_second(2)
    for which in range(2):
        put_rows(4, which, early, pairs, pairs)
    pair_copy(4).start()
    factor_pair(1, 2)
    pair_add(4)
    plane_add(3)
    factor_near(0)

    def results(p):
        x = dot(sec[0, p], ow[:half, :]) + dot(sec[1, p], ow[half:, :])
        res[p] = x.astype(BF16)

    each(4, results)
    factor_end(0, first)
    plane_add(4)
    column_add(2)
    for n in range(2):
        finish(n)
    factor_near(1)
    finish(2)
    finish_last(3)
    finish_last(4)
    factor_end(1, second)


def mega_call(nz, nx, *args):
    ns = nz * nx
    rows = 4 * ns
    width = 12 * ns
    half = width // 2
    vmem, sem = pltpu.VMEM, pltpu.SemaphoreType.DMA
    scratch = [
        vmem((4, rows, width), BF16),
        vmem((4, rows, rows), BF16),
        vmem((4, rows, rows), BF16),
        vmem((width, width), BF16),
        vmem((width, width), BF16),
        vmem((width, width), BF16),
        vmem((4, rows, width), BF16),
        vmem((width, 4 * rows), BF16),
        vmem((4, rows, rows), BF16),
        vmem((4, rows, rows), BF16),
    ]
    for sizes in ((1, 2, 3), (1, 2, 3), (3, 2, 1), (3, 2, 1)):
        scratch += [vmem((ns, 16, half // 3 * size), BF16) for size in sizes]
    scratch += [
        vmem((2, 4, rows, half), BF16),
        vmem((2, 4, rows, half), F32),
        vmem((2, 4, rows, half), F32),
        vmem((2, 4, rows, half), BF16),
        vmem((4, rows, half), F32),
        vmem((4, rows, half), BF16),
        vmem((2, 4, rows, half), BF16),
        vmem((2, 4, rows, half), BF16),
        vmem((2, 4, rows, half), BF16),
        vmem((half, 4 * rows), BF16),
        vmem((3, 4 * rows, half // 3), F32),
        vmem((2, width + 8, half), F32),
    ]
    for n in range(5):
        count, _ = zone_of(nz, n)
        scratch += [
            vmem((2, nx, count, 16, half), BF16),
            vmem((nx, count, 16, half), BF16),
            vmem((nx, count, 16, half), BF16),
            vmem((nx, count, 16, half), BF16),
            vmem((count, 16, half), BF16),
            vmem((4 * nz if n > 2 else 2 * nz, 16, half), BF16),
            vmem((2, 16, half), BF16),
        ]
    scratch += [vmem((int(nx**0.5), nz, 16, half), BF16)] * 2
    for _ in range(2):
        scratch += [
            vmem((2, 2, rows, rows), BF16),
            vmem((2, rows, rows), BF16),
            vmem((2, rows, rows), BF16),
            vmem((2, rows, rows), BF16),
            vmem((2, 2, rows, rows), BF16),
        ]
    scratch += [sem((count,)) for count in (12, 6, 6, 25, 25, 12, 12)]
    anywhere = pl.BlockSpec(memory_space=pl.ANY)
    return pl.pallas_call(
        functools.partial(mega, nz, nx),
        out_shape=(vmem((4, rows, width), BF16),) * 2
        + (vmem((4, rows, rows), F32),) * 2
        + (vmem((12, width), F32),) * 3,
        in_specs=[anywhere] * 7,
        out_specs=(pl.BlockSpec(memory_space=vmem),) * 7,
        scratch_shapes=scratch,
        compiler_params=pltpu.CompilerParams(
            collective_id=0, has_side_effects=True, vmem_limit_bytes=53 * 2**20
        ),
        cost_estimate=pl.CostEstimate(
            flops=14 * 10**9, bytes_accessed=16 * 10**6, transcendentals=10**6
        ),
        name="mixing",
    )(*args)


def deliver(*refs):
    sources, targets, sem = refs[:7], refs[7:14], refs[14]
    copies = []
    for src, dst in zip(sources, targets):
        for i in range(src.shape[0] if len(src.shape) == 3 else 1):
            pair = (src.at[i], dst.at[i]) if len(src.shape) == 3 else (src, dst)
            copies.append(pltpu.make_async_copy(*pair, sem.at[len(copies)]))
    for copy in copies:
        copy.start()
    for copy in copies:
        copy.wait()


def deliver_call(arrays):
    return pl.pallas_call(
        deliver,
        out_shape=tuple(jax.ShapeDtypeStruct(x.shape, x.dtype) for x in arrays),
        in_specs=[pl.BlockSpec(memory_space=pltpu.VMEM)] * 7,
        out_specs=(pl.BlockSpec(memory_space=pl.ANY),) * 7,
        scratch_shapes=[pltpu.SemaphoreType.DMA((19,))],
        compiler_params=pltpu.CompilerParams(vmem_limit_bytes=2**20),
        name="deliver",
    )(*arrays)


def shards(
    nz, nx, tokens, first_factor, second_factor, value_weight, gate_weight, out_weight, cotangent
):
    rows, width = 4 * nz * nx, 12 * nz * nx
    arrays = mega_call(
        nz,
        nx,
        tokens.reshape(4, rows, width),
        first_factor,
        second_factor,
        value_weight,
        gate_weight,
        out_weight,
        cotangent.reshape(4, rows, width),
    )
    result, grad, first, second, value_sum, gate_sum, out_sum = deliver_call(arrays)
    return (
        result.reshape(1, 4 * rows, width),
        grad.reshape(1, 4 * rows, width),
        first,
        second,
        value_sum,
        gate_sum,
        out_sum,
    )


def solution(mesh, nz=NZ, nx=NX):
    return jax.shard_map(
        functools.partial(shards, nz, nx),
        mesh=mesh,
        in_specs=(
            P("dp", "seq", None),
            P("seq", None, None),
            P("seq", None, None),
            P(),
            P(),
            P(),
            P("dp", "seq", None),
        ),
        out_specs=(
            P("dp", "seq", None),
            P("dp", "seq", None),
            P("seq", None, None),
            P("seq", None, None),
            P("seq", None),
            P("seq", None),
            P("seq", None),
        ),
        check_vma=False,
    )
```

```python
import functools

import jax
import jax.numpy as jnp
from jax import lax
from jax.experimental import pallas as pl
from jax.experimental.pallas import tpu as pltpu
from jax.sharding import PartitionSpec as P

MESH = pl.DeviceIdType.MESH
BF16 = jnp.bfloat16
F32 = jnp.float32
NZ, NX = 4, 16


def dot(left, right):
    return jnp.dot(left, right, preferred_element_type=F32)


def dot_cols(left, right):
    return lax.dot_general(left, right, (((1,), (1,)), ((), ())), preferred_element_type=F32)


def each(count, body):
    def step(i, carry):
        body(i)
        return carry

    lax.fori_loop(0, count, step, 0)


def zone_of(nz, n):
    return ((nz, 0), (nz, 0), (nz // 2, 0), (nz // 4, nz // 2), (nz // 4, 3 * nz // 4))[n]


def mega(nz, nx, *refs):
    ns = nz * nx
    rows = 4 * ns
    width = 12 * ns
    half = width // 2
    lanes = half // 3
    side = int(nx**0.5)
    (tok_h, ff_h, sf_h, vw_h, gw_h, ow_h, cot_h), refs = refs[:7], refs[7:]
    (res, grad, first, second), w_out, refs = refs[:4], refs[4:7], refs[7:]
    (tok, ff, sf, vw, gw, ow, cot, tok_t, ff_t, sf_t), refs = refs[:10], refs[10:]
    bsend, brecv, fsend, frecv = (refs[3 * i : 3 * i + 3] for i in range(4))
    refs = refs[12:]
    (bs, val, sig, mix), refs = refs[:4], refs[4:]
    (tmp, got, dval, dgate, sec, sec_t, term, wide), refs = refs[:8], refs[8:]
    jobs = [refs[7 * n : 7 * n + 7] for n in range(5)]
    plane_b, refs = refs[35:37], refs[37:]
    facs = [refs[5 * n : 5 * n + 5] for n in range(2)]
    refs = refs[10:]
    load_sem, a2a_send, a2a_recv, job_send, job_recv, fac_send, fac_recv = refs
    a2a, job, fac = (a2a_send, a2a_recv), (job_send, job_recv), (fac_send, fac_recv)

    dp, seq = lax.axis_index("dp"), lax.axis_index("seq")
    zl, core = dp // 2, lax.rem(dp, 2)
    zh, xy = seq // nx, lax.rem(seq, nx)
    z = zh * 2 + zl
    other = 1 - core
    partner = (zl * 2 + other, seq)
    neighbour = ((1 - zl) * 2 + core, seq)

    back_groups = ((0, 0, lanes), (0, lanes, 2 * lanes), (1, 0, half))
    parts = [(sf_h, sf)]
    for c, start, size in back_groups:
        at = pl.ds(c * half + start, size)
        parts.append((ow_h.at[at, :], ow.at[at, :]))
    parts += [(cot_h.at[p], cot.at[p]) for p in range(4)]
    parts += [(tok_h, tok), (vw_h, vw), (gw_h, gw), (ff_h, ff)]
    loads = [
        pltpu.make_async_copy(src, dst, load_sem.at[i]) for i, (src, dst) in enumerate(parts)
    ]
    for i in (1, 4, 0, 5, 6, 7):
        loads[i].start()

    barrier = pltpu.get_barrier_semaphore()

    far = sorted(range(1, nz), key=lambda dz: abs(dz - nz / 2))

    def greet(device):
        pl.semaphore_signal(barrier, inc=1, device_id=device, device_id_type=MESH)

    def greet_row(i):
        to_xy = lax.rem(xy + i, nx)
        for dz in far:
            greet((dp, lax.rem(zh + dz, nz) * nx + to_xy))

        @pl.when(i > 0)
        def _():
            greet((dp, zh * nx + to_xy))

    def greet_column(i):
        for d in range(1, 4):
            greet((lax.rem(dp + d, 4), i * nx + xy))

    each(nx, greet_row)
    each(nz, greet_column)

    def remote(src, dst, sems, k, device):
        return pltpu.make_async_remote_copy(
            src_ref=src,
            dst_ref=dst,
            send_sem=sems[0].at[k],
            recv_sem=sems[1].at[k],
            device_id=device,
            device_id_type=MESH,
        )

    def send_all(src, dst, k):
        def send(to):
            remote(src.at[to], dst.at[seq], a2a, k, (dp, to)).start()

        def row(i):
            for dz in far:
                send(lax.rem(zh + dz, nz) * nx + lax.rem(xy + i, nx))

        each(nx, row)
        each(nx - 1, lambda i: send(zh * nx + lax.rem(xy + i + 1, nx)))
        dst[seq] = src[seq]

    def all_of(src, dst, k):
        some = pl.ds(0, ns - 1)
        return remote(src.at[some], dst.at[some], a2a, k, (dp, lax.rem(seq + 1, ns)))

    def to_messages(dst, start, size):
        tiles = min(8, rows // 8)
        mask = lax.broadcasted_iota(jnp.int32, (tiles, 8, size), 1) < 4

        def block(i):
            at = pl.ds(pl.multiple_of(i * tiles * 8, 8), tiles * 8)
            r = [tmp[k, at, start : start + size].reshape(tiles, 8, size) for k in range(4)]
            turned = [pltpu.roll(x, 4, 1) for x in r]
            low = [jnp.where(mask, r[k], turned[k + 1]) for k in (0, 2)]
            high = [jnp.where(mask, turned[k], r[k + 1]) for k in (0, 2)]
            low = jnp.concatenate(low, axis=1).astype(BF16)
            high = jnp.concatenate(high, axis=1).astype(BF16)
            for t in range(tiles):
                dst[(i * tiles + t) * 2] = low[t]
                dst[(i * tiles + t) * 2 + 1] = high[t]

        each(rows // (tiles * 8), block)

    def from_messages(src, start, size):
        for j in range(size // lanes):
            cols = slice(j * lanes, (j + 1) * lanes)
            to_cols = slice(start + j * lanes, start + (j + 1) * lanes)

            def widen(i, j=j, cols=cols):
                at = pl.ds(pl.multiple_of(i * 64, 64), 64)
                part = src[pl.ds(i * 4, 4), :, cols]
                term[j, at, :] = part.reshape(64, lanes).astype(F32)

            each(4 * rows // 64, widen)
            for k in range(4):
                got[k, :, to_cols] = term[j, pl.ds(k, rows, stride=4), :].astype(BF16)

    def zone(n):
        count, base = zone_of(nz, n)
        inside = (zh >= base) & (zh < base + count)
        return count, base, inside, inside & (zl == n % 2)

    def put_rows(n, which, start, stop, offset=0):
        own = jobs[n][0]

        def two(i):
            m = start + i
            x = wide[which, pl.ds(pl.multiple_of(24 * (m + offset), 8), 32), :]
            for k in range(2):
                s = 2 * m + k
                block = x[12 * k : 12 * k + 16].astype(BF16)
                place = lax.rem(s, nx)
                if n < 2 and which == 1:
                    place = lax.rem(place, side) * side + place // side
                own[which, place, s // nx] = block

        each(stop - start, two)

    def pair_copy(n):
        return remote(jobs[n][0].at[other], jobs[n][1], job, 5 * n, partner)

    def pair_add(n):
        own, pair, u, plane = jobs[n][:4]
        pair_copy(n).wait()

        def add(i):
            u[i] = (own[core, i].astype(F32) + pair[i].astype(F32)).astype(BF16)

        each(nx, add)
        if n < 2:

            def send_side(i):
                to = lax.rem(mine + i + 1, side)
                src, dst = u.at[pl.ds(to * side, side)], plane.at[pl.ds(mine * side, side)]
                remote(src, dst, job, 5 * n + 1, along(to, crossed)).start()

            each(side - 1, send_side)

            def keep(i):
                plane[mine * side + i] = u[mine * side + i]

            each(side, keep)
        else:

            def send(i):
                to = lax.rem(xy + i + 1, nx)
                remote(u.at[to], plane.at[xy], job, 5 * n + 1, (dp, zh * nx + to)).start()

            each(nx - 1, send)
            plane[xy] = u[xy]

    mine = (1 - core) * (xy // side) + core * lax.rem(xy, side)
    crossed = core * (xy // side) + (1 - core) * lax.rem(xy, side)

    def along(at_mine, at_crossed):
        place = (1 - core) * (at_mine * side + at_crossed) + core * (at_crossed * side + at_mine)
        return dp, zh * nx + place

    def side_add(n):
        u, plane = jobs[n][2:4]
        some = pl.ds(0, (side - 1) * side)
        remote(u.at[some], plane.at[some], job, 5 * n + 1, partner).wait()

        def add(i):
            x = plane[i].astype(F32)
            for k in range(1, side):
                x = x + plane[k * side + i].astype(F32)
            u[i] = x.astype(BF16)

        each(side, add)

        def send(i):
            to = lax.rem(crossed + i + 1, side)
            remote(
                u.at[to], plane_b[n].at[crossed], job, 5 * n + 4, along(mine, to)
            ).start()

        each(side - 1, send)
        plane_b[n][crossed] = u[crossed]

    def plane_add(n):
        u, plane, total, col = jobs[n][2:6]
        count, base, inside, member = zone(n)
        if n < 2:
            some = pl.ds(0, side - 1)
            plane, sources = plane_b[n], side
            remote(u.at[some], plane.at[some], job, 5 * n + 4, partner).wait()
        else:
            some, sources = pl.ds(0, nx - 1), nx
            remote(u.at[some], plane.at[some], job, 5 * n + 1, partner).wait()

        def add(q):
            x = plane[0, q].astype(F32)
            for i in range(1, sources):
                x = x + plane[i, q].astype(F32)
            total[q] = x.astype(BF16)

        each(count, add)
        if n < 3:

            def send(i):
                @pl.when((base + i != zh) | (zl != n % 2))
                def _():
                    device = ((n % 2) * 2 + core, (base + i) * nx + xy)
                    remote(total.at[i], col.at[z], job, 5 * n + 2, device).start()

            each(count, send)

            @pl.when(member)
            def _():
                col[z] = total[zh - base]

        else:

            def send(i):
                to_dp = lax.rem(i, 4)

                @pl.when((base + i // 4 != zh) | (to_dp != dp))
                def _():
                    device = (to_dp, (base + i // 4) * nx + xy)
                    slot = col.at[core * 2 * nz + z]
                    remote(total.at[i // 4], slot, job, 5 * n + 2, device).start()

            each(4 * count, send)

            @pl.when(inside)
            def _():
                col[core * 2 * nz + z] = total[zh - base]

    def pieces(n, sem, size):
        some = pl.ds(0, size)
        return remote(jobs[n][5].at[some], jobs[n][5].at[some], job, 5 * n + sem, partner)

    def sum_of(col, start):
        x = col[start].astype(F32)
        for i in range(1, 2 * nz):
            x = x + col[start + i].astype(F32)
        return x

    def column_add(n):
        col, fin = jobs[n][5:]
        count, _, _, member = zone(n)

        @pl.when(member)
        def _():
            pieces(n, 2, 2 * nz - 1).wait_recv()
            fin[core] = sum_of(col, 0).astype(BF16)
            for d in range(1, 4):
                device = (lax.rem(dp + d, 4), seq)
                remote(fin.at[core], fin.at[core], job, 5 * n + 3, device).start()
            pieces(n, 2, count - 1).wait_send()

        @pl.when(jnp.logical_not(member))
        def _():
            pieces(n, 2, count).wait_send()

    def finish(n):
        fin = jobs[n][6]
        _, _, inside, member = zone(n)

        @pl.when(inside)
        def _():
            @pl.when(member)
            def _():
                remote(fin.at[other], fin.at[other], job, 5 * n + 3, partner).wait_recv()
                pieces(n, 3, 3).wait_send()

            @pl.when(jnp.logical_not(member))
            def _():
                remote(fin, fin, job, 5 * n + 3, partner).wait_recv()

            at = [
                ((0, slice(0, half)), (1, slice(0, half))),
                ((0, slice(half, width)), (1, slice(half, width))),
                ((2, slice(0, half)), (2, slice(half, width))),
            ][n]
            for k in range(2):
                w_out[at[k][0]][:, at[k][1]] = fin[k].astype(F32)[:12]

    def finish_last(n):
        col = jobs[n][5]
        count, _, inside, _ = zone(n)

        @pl.when(inside)
        def _():
            pieces(n, 2, 4 * nz - 1).wait_recv()
            for k in range(2):
                total = sum_of(col, 2 * nz * k).astype(BF16)
                w_out[2][:, k * half : (k + 1) * half] = total.astype(F32)[:12]
            pieces(n, 2, 4 * count - 1).wait_send()

        @pl.when(jnp.logical_not(inside))
        def _():
            pieces(n, 2, 4 * count).wait_send()

    def factor_copy(n, k):
        own, pair = facs[n][:2]
        return remote(own.at[other, k], pair.at[k], fac, 6 * n + k, partner)

    def factor_start(n, source, before=None):
        own = facs[n][0]
        for k in range(2):
            for h in range(2):
                if before is not None:
                    before(2 * h + k)
                own[h, k] = source[2 * h + k].astype(BF16)
            factor_copy(n, k).start()

    def factor_pair(n, send):
        own, pair, u = facs[n][:3]
        for k in range(2):
            factor_copy(n, k).wait()
            u[k] = (own[core, k].astype(F32) + pair[k].astype(F32)).astype(BF16)
            if k < send:
                near_copy(n, k).start()

    def near_copy(n, k):
        return remote(facs[n][2].at[k], facs[n][3].at[k], fac, 6 * n + 2 + k, neighbour)

    def fin_copy(n, k):
        fin = facs[n][4]
        return remote(fin.at[core, k], fin.at[core, k], fac, 6 * n + 4 + k, partner)

    def factor_near(n):
        _, _, u, near, fin = facs[n]
        for k in range(2):
            near_copy(n, k).wait()
            fin[core, k] = (u[k].astype(F32) + near[k].astype(F32)).astype(BF16)
            fin_copy(n, k).start()

    def factor_end(n, wide_sum):
        fin = facs[n][4]
        for k in range(2):
            fin_copy(n, k).wait()
        for k in range(4):
            wide_sum[k] = fin[k // 2, k % 2].astype(F32)

    for which in range(2):
        wide[which, width:, :] = jnp.zeros((8, half), F32)

    for g, (c, start, size) in enumerate(back_groups):
        loads[1 + g].wait()

        def back(p, c=c, start=start, size=size):
            at = c * half + start
            part = dot_cols(cot[p], ow[at : at + size, :]).astype(BF16)
            bs[c, p, :, start : start + size] = part
            tmp[p, :, :size] = dot(sf_t[p], part)

        if g == 0:
            loads[0].wait()
            for p in range(4):
                sf_t[p] = sf[p].T
                loads[4 + p].wait()
                if p == 1:
                    for load in loads[2:4] + loads[8:]:
                        load.start()
                back(p)
        else:
            each(4, back)
        to_messages(bsend[g], 0, size)
        if g == 0:
            pl.semaphore_wait(barrier, ns - 1 + 3 * nz)
        send_all(bsend[g], brecv[g], g)

    for load in loads[8:]:
        load.wait()
    forward_groups = ((0, 0, half), (1, 0, 2 * lanes), (1, 2 * lanes, lanes))
    for c in range(2):
        cols = slice(c * half, (c + 1) * half)

        def forward(a, c=c, cols=cols):
            v = dot(tok[a], vw[:, cols])
            s = jax.nn.sigmoid(dot(tok[a], gw[:, cols]))
            m = (v * s).astype(BF16)
            val[c, a] = v
            sig[c, a] = s
            mix[c, a] = m
            tmp[a] = dot(ff[a], m)

        each(4, forward)
        for g, (group_c, start, size) in enumerate(forward_groups):
            if group_c == c:
                to_messages(fsend[g], start, size)
    for k in range(4):
        ff_t[k] = ff[k].T
        tok_t[:, k * rows : (k + 1) * rows] = tok[k].T

    def back_copy(g):
        return all_of(bsend[g], brecv[g], g)

    def forward_copy(g):
        return all_of(fsend[g], frecv[g], 3 + g)

    for c in range(2):
        groups = [g for g in range(3) if back_groups[g][0] == c]
        if c == 1:
            pair_add(0)
        for g in groups:
            back_copy(g).wait_send()
        for g in range(3):
            if forward_groups[g][0] == c:
                send_all(fsend[g], frecv[g], 3 + g)
        for g in groups:
            back_copy(g).wait_recv()
            from_messages(brecv[g], *back_groups[g][1:])

        def inner(a, c=c):
            g = got[a]
            part = dot(ff_t[a], g)
            s = sig[c, a]
            ps = part * s
            dval[c, a] = ps.astype(BF16)
            dgate[c, a] = (ps * val[c, a] * (1.0 - s)).astype(BF16)
            more = dot_cols(g, mix[c, a])
            if c == 0:
                first[a] = more
            else:
                first[a] = first[a] + more

        each(4, inner)
        for which, source in enumerate((dval, dgate)):

            def terms(m, c=c, which=which, source=source):
                at = pl.ds(pl.multiple_of(m * rows, 8), rows)
                wide[which, at, :] = dot(tok_t[at, :], source[c].reshape(4 * rows, half))

            each(3, terms)
            put_rows(c, which, 0, ns // 2)
        pair_copy(c).start()
    factor_start(0, first)
    side_add(0)
    pair_add(1)
    factor_pair(0, 1)

    def grads(a):
        x = dot_cols(dval[0, a], vw[:, :half]) + dot_cols(dval[1, a], vw[:, half:])
        y = dot_cols(dgate[0, a], gw[:, :half]) + dot_cols(dgate[1, a], gw[:, half:])
        grad[a] = (x + y).astype(BF16)

    each(4, grads)
    plane_add(0)
    side_add(1)

    def take(g):
        forward_copy(g).wait_recv()
        from_messages(frecv[g], *forward_groups[g][1:])

    def mix_second(g):
        c, start, size = forward_groups[g]
        cols = slice(start, start + size)
        def inner(p):
            sec[c, p, :, cols] = dot(sf[p], got[p, :, cols]).astype(BF16)

        each(4, inner)
        for k in range(4):
            sec_t[cols, k * rows : (k + 1) * rows] = sec[c, k, :, cols].T
        for which in range(2):
            right = cot[:, :, which * half : (which + 1) * half].reshape(4 * rows, half)
            wide[which, cols, :] = dot(sec_t[cols, :], right)

    def grow(g, p):
        c, start, size = forward_groups[g]
        cols = slice(start, start + size)
        more = dot_cols(bs[c, p, :, cols], got[p, :, cols])
        if g == 0:
            second[p] = more
        else:
            second[p] = second[p] + more

    def grow_second(g):
        each(4, functools.partial(grow, g))

    take(0)
    mix_second(0)
    for which in range(2):
        put_rows(2, which, 0, ns // 4)
    pair_copy(2).start()
    grow_second(0)
    plane_add(1)
    pair_add(2)
    pairs = ns // 8
    early = 2 * lanes // 24 - pairs
    take(1)
    mix_second(1)
    for which in range(2):
        put_rows(3, which, 0, pairs)
    pair_copy(3).start()
    for which in range(2):
        put_rows(4, which, 0, early, pairs)
    grow_second(1)
    pair_add(3)
    for g in range(3):
        forward_copy(g).wait_send()
    near_copy(0, 1).start()
    plane_add(2)
    column_add(0)
    column_add(1)
    take(2)
    factor_start(1, second, functools.partial(grow, 2))
    mix_second(2)
    for which in range(2):
        put_rows(4, which, early, pairs, pairs)
    pair_copy(4).start()
    factor_pair(1, 2)
    pair_add(4)
    plane_add(3)
    factor_near(0)

    def results(p):
        x = dot(sec[0, p], ow[:half, :]) + dot(sec[1, p], ow[half:, :])
        res[p] = x.astype(BF16)

    each(4, results)
    factor_end(0, first)
    plane_add(4)
    column_add(2)
    for n in range(2):
        finish(n)
    factor_near(1)
    finish(2)
    finish_last(3)
    finish_last(4)
    factor_end(1, second)


def mega_call(nz, nx, *args):
    ns = nz * nx
    rows = 4 * ns
    width = 12 * ns
    half = width // 2
    vmem, sem = pltpu.VMEM, pltpu.SemaphoreType.DMA
    scratch = [
        vmem((4, rows, width), BF16),
        vmem((4, rows, rows), BF16),
        vmem((4, rows, rows), BF16),
        vmem((width, width), BF16),
        vmem((width, width), BF16),
        vmem((width, width), BF16),
        vmem((4, rows, width), BF16),
        vmem((width, 4 * rows), BF16),
        vmem((4, rows, rows), BF16),
        vmem((4, rows, rows), BF16),
    ]
    for sizes in ((1, 2, 3), (1, 2, 3), (3, 2, 1), (3, 2, 1)):
        scratch += [vmem((ns, 16, half // 3 * size), BF16) for size in sizes]
    scratch += [
        vmem((2, 4, rows, half), BF16),
        vmem((2, 4, rows, half), F32),
        vmem((2, 4, rows, half), F32),
        vmem((2, 4, rows, half), BF16),
        vmem((4, rows, half), F32),
        vmem((4, rows, half), BF16),
        vmem((2, 4, rows, half), BF16),
        vmem((2, 4, rows, half), BF16),
        vmem((2, 4, rows, half), BF16),
        vmem((half, 4 * rows), BF16),
        vmem((3, 4 * rows, half // 3), F32),
        vmem((2, width + 8, half), F32),
    ]
    for n in range(5):
        count, _ = zone_of(nz, n)
        scratch += [
            vmem((2, nx, count, 16, half), BF16),
            vmem((nx, count, 16, half), BF16),
            vmem((nx, count, 16, half), BF16),
            vmem((nx, count, 16, half), BF16),
            vmem((count, 16, half), BF16),
            vmem((4 * nz if n > 2 else 2 * nz, 16, half), BF16),
            vmem((2, 16, half), BF16),
        ]
    scratch += [vmem((int(nx**0.5), nz, 16, half), BF16)] * 2
    for _ in range(2):
        scratch += [
            vmem((2, 2, rows, rows), BF16),
            vmem((2, rows, rows), BF16),
            vmem((2, rows, rows), BF16),
            vmem((2, rows, rows), BF16),
            vmem((2, 2, rows, rows), BF16),
        ]
    scratch += [sem((count,)) for count in (12, 6, 6, 25, 25, 12, 12)]
    anywhere = pl.BlockSpec(memory_space=pl.ANY)
    return pl.pallas_call(
        functools.partial(mega, nz, nx),
        out_shape=(vmem((4, rows, width), BF16),) * 2
        + (vmem((4, rows, rows), F32),) * 2
        + (vmem((12, width), F32),) * 3,
        in_specs=[anywhere] * 7,
        out_specs=(pl.BlockSpec(memory_space=vmem),) * 7,
        scratch_shapes=scratch,
        compiler_params=pltpu.CompilerParams(
            collective_id=0, has_side_effects=True, vmem_limit_bytes=53 * 2**20
        ),
        cost_estimate=pl.CostEstimate(
            flops=14 * 10**9, bytes_accessed=16 * 10**6, transcendentals=10**6
        ),
        name="mixing",
    )(*args)


def deliver(*refs):
    sources, targets, sem = refs[:7], refs[7:14], refs[14]
    copies = []
    for src, dst in zip(sources, targets):
        for i in range(src.shape[0] if len(src.shape) == 3 else 1):
            pair = (src.at[i], dst.at[i]) if len(src.shape) == 3 else (src, dst)
            copies.append(pltpu.make_async_copy(*pair, sem.at[len(copies)]))
    for copy in copies:
        copy.start()
    for copy in copies:
        copy.wait()


def deliver_call(arrays):
    return pl.pallas_call(
        deliver,
        out_shape=tuple(jax.ShapeDtypeStruct(x.shape, x.dtype) for x in arrays),
        in_specs=[pl.BlockSpec(memory_space=pltpu.VMEM)] * 7,
        out_specs=(pl.BlockSpec(memory_space=pl.ANY),) * 7,
        scratch_shapes=[pltpu.SemaphoreType.DMA((19,))],
        compiler_params=pltpu.CompilerParams(vmem_limit_bytes=2**20),
        name="deliver",
    )(*arrays)


def shards(
    nz, nx, tokens, first_factor, second_factor, value_weight, gate_weight, out_weight, cotangent
):
    rows, width = 4 * nz * nx, 12 * nz * nx
    arrays = mega_call(
        nz,
        nx,
        tokens.reshape(4, rows, width),
        first_factor,
        second_factor,
        value_weight,
        gate_weight,
        out_weight,
        cotangent.reshape(4, rows, width),
    )
    result, grad, first, second, value_sum, gate_sum, out_sum = deliver_call(arrays)
    return (
        result.reshape(1, 4 * rows, width),
        grad.reshape(1, 4 * rows, width),
        first,
        second,
        value_sum,
        gate_sum,
        out_sum,
    )


def solution(mesh, nz=NZ, nx=NX):
    return jax.shard_map(
        functools.partial(shards, nz, nx),
        mesh=mesh,
        in_specs=(
            P("dp", "seq", None),
            P("seq", None, None),
            P("seq", None, None),
            P(),
            P(),
            P(),
            P("dp", "seq", None),
        ),
        out_specs=(
            P("dp", "seq", None),
            P("dp", "seq", None),
            P("seq", None, None),
            P("seq", None, None),
            P("seq", None),
            P("seq", None),
            P("seq", None),
        ),
        check_vma=False,
    )
```

```python
import functools

import jax
import jax.numpy as jnp
from jax import lax
from jax.experimental import pallas as pl
from jax.experimental.pallas import tpu as pltpu
from jax.sharding import PartitionSpec as P

MESH = pl.DeviceIdType.MESH
BF16 = jnp.bfloat16
F32 = jnp.float32
NZ, NX = 4, 16


def dot(left, right):
    return jnp.dot(left, right, preferred_element_type=F32)


def dot_cols(left, right):
    return lax.dot_general(left, right, (((1,), (1,)), ((), ())), preferred_element_type=F32)


def each(count, body):
    def step(i, carry):
        body(i)
        return carry

    lax.fori_loop(0, count, step, 0)


def zone_of(nz, n):
    return ((nz, 0), (nz, 0), (nz // 2, 0), (nz // 4, nz // 2), (nz // 4, 3 * nz // 4))[n]


def mega(nz, nx, *refs):
    ns = nz * nx
    rows = 4 * ns
    width = 12 * ns
    half = width // 2
    lanes = half // 3
    side = int(nx**0.5)
    (tok_h, ff_h, sf_h, vw_h, gw_h, ow_h, cot_h), refs = refs[:7], refs[7:]
    (res, grad, first, second), w_out, refs = refs[:4], refs[4:7], refs[7:]
    (tok, ff, sf, vw, gw, ow, cot, tok_t, ff_t, sf_t), refs = refs[:10], refs[10:]
    bsend, brecv, fsend, frecv = (refs[3 * i : 3 * i + 3] for i in range(4))
    refs = refs[12:]
    (bs, val, sig, mix), refs = refs[:4], refs[4:]
    (tmp, got, dval, dgate, sec, sec_t, term, wide), refs = refs[:8], refs[8:]
    jobs = [refs[7 * n : 7 * n + 7] for n in range(5)]
    plane_b, refs = refs[35:37], refs[37:]
    facs = [refs[5 * n : 5 * n + 5] for n in range(2)]
    refs = refs[10:]
    load_sem, a2a_send, a2a_recv, job_send, job_recv, fac_send, fac_recv = refs
    a2a, job, fac = (a2a_send, a2a_recv), (job_send, job_recv), (fac_send, fac_recv)

    dp, seq = lax.axis_index("dp"), lax.axis_index("seq")
    zl, core = dp // 2, lax.rem(dp, 2)
    zh, xy = seq // nx, lax.rem(seq, nx)
    z = zh * 2 + zl
    other = 1 - core
    partner = (zl * 2 + other, seq)
    neighbour = ((1 - zl) * 2 + core, seq)

    back_groups = ((0, 0, lanes), (0, lanes, 2 * lanes), (1, 0, half))
    parts = [(sf_h, sf)]
    for c, start, size in back_groups:
        at = pl.ds(c * half + start, size)
        parts.append((ow_h.at[at, :], ow.at[at, :]))
    parts += [(cot_h.at[p], cot.at[p]) for p in range(4)]
    parts += [(tok_h, tok), (vw_h, vw), (gw_h, gw), (ff_h, ff)]
    loads = [
        pltpu.make_async_copy(src, dst, load_sem.at[i]) for i, (src, dst) in enumerate(parts)
    ]
    for i in (1, 4, 0, 5, 6, 7):
        loads[i].start()

    barrier = pltpu.get_barrier_semaphore()

    far = sorted(range(1, nz), key=lambda dz: abs(dz - nz / 2))

    def greet(device):
        pl.semaphore_signal(barrier, inc=1, device_id=device, device_id_type=MESH)

    def greet_row(i):
        to_xy = lax.rem(xy + i, nx)
        for dz in far:
            greet((dp, lax.rem(zh + dz, nz) * nx + to_xy))

        @pl.when(i > 0)
        def _():
            greet((dp, zh * nx + to_xy))

    def greet_column(i):
        for d in range(1, 4):
            greet((lax.rem(dp + d, 4), i * nx + xy))

    each(nx, greet_row)
    each(nz, greet_column)

    def remote(src, dst, sems, k, device):
        return pltpu.make_async_remote_copy(
            src_ref=src,
            dst_ref=dst,
            send_sem=sems[0].at[k],
            recv_sem=sems[1].at[k],
            device_id=device,
            device_id_type=MESH,
        )

    def send_all(src, dst, k):
        def send(to):
            remote(src.at[to], dst.at[seq], a2a, k, (dp, to)).start()

        def row(i):
            for dz in far:
                send(lax.rem(zh + dz, nz) * nx + lax.rem(xy + i, nx))

        each(nx, row)
        each(nx - 1, lambda i: send(zh * nx + lax.rem(xy + i + 1, nx)))
        dst[seq] = src[seq]

    def all_of(src, dst, k):
        some = pl.ds(0, ns - 1)
        return remote(src.at[some], dst.at[some], a2a, k, (dp, lax.rem(seq + 1, ns)))

    def to_messages(dst, start, size):
        tiles = min(8, rows // 8)
        mask = lax.broadcasted_iota(jnp.int32, (tiles, 8, size), 1) < 4

        def block(i):
            at = pl.ds(pl.multiple_of(i * tiles * 8, 8), tiles * 8)
            r = [tmp[k, at, start : start + size].reshape(tiles, 8, size) for k in range(4)]
            turned = [pltpu.roll(x, 4, 1) for x in r]
            low = [jnp.where(mask, r[k], turned[k + 1]) for k in (0, 2)]
            high = [jnp.where(mask, turned[k], r[k + 1]) for k in (0, 2)]
            low = jnp.concatenate(low, axis=1).astype(BF16)
            high = jnp.concatenate(high, axis=1).astype(BF16)
            for t in range(tiles):
                dst[(i * tiles + t) * 2] = low[t]
                dst[(i * tiles + t) * 2 + 1] = high[t]

        each(rows // (tiles * 8), block)

    def from_messages(src, start, size):
        for j in range(size // lanes):
            cols = slice(j * lanes, (j + 1) * lanes)
            to_cols = slice(start + j * lanes, start + (j + 1) * lanes)

            def widen(i, j=j, cols=cols):
                at = pl.ds(pl.multiple_of(i * 64, 64), 64)
                part = src[pl.ds(i * 4, 4), :, cols]
                term[j, at, :] = part.reshape(64, lanes).astype(F32)

            each(4 * rows // 64, widen)
            for k in range(4):
                got[k, :, to_cols] = term[j, pl.ds(k, rows, stride=4), :].astype(BF16)

    def zone(n):
        count, base = zone_of(nz, n)
        inside = (zh >= base) & (zh < base + count)
        return count, base, inside, inside & (zl == n % 2)

    def put_rows(n, which, start, stop, offset=0):
        own = jobs[n][0]

        def two(i):
            m = start + i
            x = wide[which, pl.ds(pl.multiple_of(24 * (m + offset), 8), 32), :]
            for k in range(2):
                s = 2 * m + k
                block = x[12 * k : 12 * k + 16].astype(BF16)
                place = lax.rem(s, nx)
                if n < 2 and which == 1:
                    place = lax.rem(place, side) * side + place // side
                own[which, place, s // nx] = block

        each(stop - start, two)

    def pair_copy(n):
        return remote(jobs[n][0].at[other], jobs[n][1], job, 5 * n, partner)

    def pair_add(n):
        own, pair, u, plane = jobs[n][:4]
        pair_copy(n).wait()

        def add(i):
            u[i] = (own[core, i].astype(F32) + pair[i].astype(F32)).astype(BF16)

        each(nx, add)
        if n < 2:

            def send_side(i):
                to = lax.rem(mine + i + 1, side)
                src, dst = u.at[pl.ds(to * side, side)], plane.at[pl.ds(mine * side, side)]
                remote(src, dst, job, 5 * n + 1, along(to, crossed)).start()

            each(side - 1, send_side)

            def keep(i):
                plane[mine * side + i] = u[mine * side + i]

            each(side, keep)
        else:

            def send(i):
                to = lax.rem(xy + i + 1, nx)
                remote(u.at[to], plane.at[xy], job, 5 * n + 1, (dp, zh * nx + to)).start()

            each(nx - 1, send)
            plane[xy] = u[xy]

    mine = (1 - core) * (xy // side) + core * lax.rem(xy, side)
    crossed = core * (xy // side) + (1 - core) * lax.rem(xy, side)

    def along(at_mine, at_crossed):
        place = (1 - core) * (at_mine * side + at_crossed) + core * (at_crossed * side + at_mine)
        return dp, zh * nx + place

    def side_add(n):
        u, plane = jobs[n][2:4]
        some = pl.ds(0, (side - 1) * side)
        remote(u.at[some], plane.at[some], job, 5 * n + 1, partner).wait()

        def add(i):
            x = plane[i].astype(F32)
            for k in range(1, side):
                x = x + plane[k * side + i].astype(F32)
            u[i] = x.astype(BF16)

        each(side, add)

        def send(i):
            to = lax.rem(crossed + i + 1, side)
            remote(
                u.at[to], plane_b[n].at[crossed], job, 5 * n + 4, along(mine, to)
            ).start()

        each(side - 1, send)
        plane_b[n][crossed] = u[crossed]

    def plane_add(n):
        u, plane, total, col = jobs[n][2:6]
        count, base, inside, member = zone(n)
        if n < 2:
            some = pl.ds(0, side - 1)
            plane, sources = plane_b[n], side
            remote(u.at[some], plane.at[some], job, 5 * n + 4, partner).wait()
        else:
            some, sources = pl.ds(0, nx - 1), nx
            remote(u.at[some], plane.at[some], job, 5 * n + 1, partner).wait()

        def add(q):
            x = plane[0, q].astype(F32)
            for i in range(1, sources):
                x = x + plane[i, q].astype(F32)
            total[q] = x.astype(BF16)

        each(count, add)
        if n < 3:

            def send(i):
                @pl.when((base + i != zh) | (zl != n % 2))
                def _():
                    device = ((n % 2) * 2 + core, (base + i) * nx + xy)
                    remote(total.at[i], col.at[z], job, 5 * n + 2, device).start()

            each(count, send)

            @pl.when(member)
            def _():
                col[z] = total[zh - base]

        else:

            def send(i):
                to_dp = lax.rem(i, 4)

                @pl.when((base + i // 4 != zh) | (to_dp != dp))
                def _():
                    device = (to_dp, (base + i // 4) * nx + xy)
                    slot = col.at[core * 2 * nz + z]
                    remote(total.at[i // 4], slot, job, 5 * n + 2, device).start()

            each(4 * count, send)

            @pl.when(inside)
            def _():
                col[core * 2 * nz + z] = total[zh - base]

    def pieces(n, sem, size):
        some = pl.ds(0, size)
        return remote(jobs[n][5].at[some], jobs[n][5].at[some], job, 5 * n + sem, partner)

    def sum_of(col, start):
        x = col[start].astype(F32)
        for i in range(1, 2 * nz):
            x = x + col[start + i].astype(F32)
        return x

    def column_add(n):
        col, fin = jobs[n][5:]
        count, _, _, member = zone(n)

        @pl.when(member)
        def _():
            pieces(n, 2, 2 * nz - 1).wait_recv()
            fin[core] = sum_of(col, 0).astype(BF16)
            for d in range(1, 4):
                device = (lax.rem(dp + d, 4), seq)
                remote(fin.at[core], fin.at[core], job, 5 * n + 3, device).start()
            pieces(n, 2, count - 1).wait_send()

        @pl.when(jnp.logical_not(member))
        def _():
            pieces(n, 2, count).wait_send()

    def finish(n):
        fin = jobs[n][6]
        _, _, inside, member = zone(n)

        @pl.when(inside)
        def _():
            @pl.when(member)
            def _():
                remote(fin.at[other], fin.at[other], job, 5 * n + 3, partner).wait_recv()
                pieces(n, 3, 3).wait_send()

            @pl.when(jnp.logical_not(member))
            def _():
                remote(fin, fin, job, 5 * n + 3, partner).wait_recv()

            at = [
                ((0, slice(0, half)), (1, slice(0, half))),
                ((0, slice(half, width)), (1, slice(half, width))),
                ((2, slice(0, half)), (2, slice(half, width))),
            ][n]
            for k in range(2):
                w_out[at[k][0]][:, at[k][1]] = fin[k].astype(F32)[:12]

    def finish_last(n):
        col = jobs[n][5]
        count, _, inside, _ = zone(n)

        @pl.when(inside)
        def _():
            pieces(n, 2, 4 * nz - 1).wait_recv()
            for k in range(2):
                total = sum_of(col, 2 * nz * k).astype(BF16)
                w_out[2][:, k * half : (k + 1) * half] = total.astype(F32)[:12]
            pieces(n, 2, 4 * count - 1).wait_send()

        @pl.when(jnp.logical_not(inside))
        def _():
            pieces(n, 2, 4 * count).wait_send()

    def factor_copy(n, k):
        own, pair = facs[n][:2]
        return remote(own.at[other, k], pair.at[k], fac, 6 * n + k, partner)

    def factor_start(n, source, before=None):
        own = facs[n][0]
        for k in range(2):
            for h in range(2):
                if before is not None:
                    before(2 * h + k)
                own[h, k] = source[2 * h + k].astype(BF16)
            factor_copy(n, k).start()

    def factor_pair(n, send):
        own, pair, u = facs[n][:3]
        for k in range(2):
            factor_copy(n, k).wait()
            u[k] = (own[core, k].astype(F32) + pair[k].astype(F32)).astype(BF16)
            if k < send:
                near_copy(n, k).start()

    def near_copy(n, k):
        return remote(facs[n][2].at[k], facs[n][3].at[k], fac, 6 * n + 2 + k, neighbour)

    def fin_copy(n, k):
        fin = facs[n][4]
        return remote(fin.at[core, k], fin.at[core, k], fac, 6 * n + 4 + k, partner)

    def factor_near(n):
        _, _, u, near, fin = facs[n]
        for k in range(2):
            near_copy(n, k).wait()
            fin[core, k] = (u[k].astype(F32) + near[k].astype(F32)).astype(BF16)
            fin_copy(n, k).start()

    def factor_end(n, wide_sum):
        fin = facs[n][4]
        for k in range(2):
            fin_copy(n, k).wait()
        for k in range(4):
            wide_sum[k] = fin[k // 2, k % 2].astype(F32)

    for which in range(2):
        wide[which, width:, :] = jnp.zeros((8, half), F32)

    for g, (c, start, size) in enumerate(back_groups):
        loads[1 + g].wait()

        def back(p, c=c, start=start, size=size):
            at = c * half + start
            part = dot_cols(cot[p], ow[at : at + size, :]).astype(BF16)
            bs[c, p, :, start : start + size] = part
            tmp[p, :, :size] = dot(sf_t[p], part)

        if g == 0:
            loads[0].wait()
            for p in range(4):
                sf_t[p] = sf[p].T
                loads[4 + p].wait()
                if p == 1:
                    for load in loads[2:4] + loads[8:]:
                        load.start()
                back(p)
        else:
            each(4, back)
        to_messages(bsend[g], 0, size)
        if g == 0:
            pl.semaphore_wait(barrier, ns - 1 + 3 * nz)
        send_all(bsend[g], brecv[g], g)

    for load in loads[8:]:
        load.wait()
    forward_groups = ((0, 0, half), (1, 0, 2 * lanes), (1, 2 * lanes, lanes))
    for c in range(2):
        cols = slice(c * half, (c + 1) * half)

        def forward(a, c=c, cols=cols):
            v = dot(tok[a], vw[:, cols])
            s = jax.nn.sigmoid(dot(tok[a], gw[:, cols]))
            m = (v * s).astype(BF16)
            val[c, a] = v
            sig[c, a] = s
            mix[c, a] = m
            tmp[a] = dot(ff[a], m)

        each(4, forward)
        for g, (group_c, start, size) in enumerate(forward_groups):
            if group_c == c:
                to_messages(fsend[g], start, size)
    for k in range(4):
        ff_t[k] = ff[k].T
        tok_t[:, k * rows : (k + 1) * rows] = tok[k].T

    def back_copy(g):
        return all_of(bsend[g], brecv[g], g)

    def forward_copy(g):
        return all_of(fsend[g], frecv[g], 3 + g)

    for c in range(2):
        groups = [g for g in range(3) if back_groups[g][0] == c]
        if c == 1:
            pair_add(0)
        for g in groups:
            back_copy(g).wait_send()
        for g in range(3):
            if forward_groups[g][0] == c:
                send_all(fsend[g], frecv[g], 3 + g)
        for g in groups:
            back_copy(g).wait_recv()
            from_messages(brecv[g], *back_groups[g][1:])

        def inner(a, c=c):
            g = got[a]
            part = dot(ff_t[a], g)
            s = sig[c, a]
            ps = part * s
            dval[c, a] = ps.astype(BF16)
            dgate[c, a] = (ps * val[c, a] * (1.0 - s)).astype(BF16)
            more = dot_cols(g, mix[c, a])
            if c == 0:
                first[a] = more
            else:
                first[a] = first[a] + more

        each(4, inner)
        for which, source in enumerate((dval, dgate)):

            def terms(m, c=c, which=which, source=source):
                at = pl.ds(pl.multiple_of(m * rows, 8), rows)
                wide[which, at, :] = dot(tok_t[at, :], source[c].reshape(4 * rows, half))

            each(3, terms)
            put_rows(c, which, 0, ns // 2)
        pair_copy(c).start()
    factor_start(0, first)
    side_add(0)
    pair_add(1)
    factor_pair(0, 1)

    def grads(a):
        x = dot_cols(dval[0, a], vw[:, :half]) + dot_cols(dval[1, a], vw[:, half:])
        y = dot_cols(dgate[0, a], gw[:, :half]) + dot_cols(dgate[1, a], gw[:, half:])
        grad[a] = (x + y).astype(BF16)

    each(4, grads)
    plane_add(0)
    side_add(1)

    def take(g):
        forward_copy(g).wait_recv()
        from_messages(frecv[g], *forward_groups[g][1:])

    def mix_second(g):
        c, start, size = forward_groups[g]
        cols = slice(start, start + size)
        def inner(p):
            sec[c, p, :, cols] = dot(sf[p], got[p, :, cols]).astype(BF16)

        each(4, inner)
        for k in range(4):
            sec_t[cols, k * rows : (k + 1) * rows] = sec[c, k, :, cols].T
        for which in range(2):
            right = cot[:, :, which * half : (which + 1) * half].reshape(4 * rows, half)
            wide[which, cols, :] = dot(sec_t[cols, :], right)

    def grow(g, p):
        c, start, size = forward_groups[g]
        cols = slice(start, start + size)
        more = dot_cols(bs[c, p, :, cols], got[p, :, cols])
        if g == 0:
            second[p] = more
        else:
            second[p] = second[p] + more

    def grow_second(g):
        each(4, functools.partial(grow, g))

    take(0)
    mix_second(0)
    for which in range(2):
        put_rows(2, which, 0, ns // 4)
    pair_copy(2).start()
    grow_second(0)
    plane_add(1)
    pair_add(2)
    pairs = ns // 8
    early = 2 * lanes // 24 - pairs
    take(1)
    mix_second(1)
    for which in range(2):
        put_rows(3, which, 0, pairs)
    pair_copy(3).start()
    for which in range(2):
        put_rows(4, which, 0, early, pairs)
    grow_second(1)
    pair_add(3)
    for g in range(3):
        forward_copy(g).wait_send()
    near_copy(0, 1).start()
    plane_add(2)
    column_add(0)
    column_add(1)
    take(2)
    factor_start(1, second, functools.partial(grow, 2))
    mix_second(2)
    for which in range(2):
        put_rows(4, which, early, pairs, pairs)
    pair_copy(4).start()
    factor_pair(1, 2)
    pair_add(4)
    plane_add(3)
    factor_near(0)

    def results(p):
        x = dot(sec[0, p], ow[:half, :]) + dot(sec[1, p], ow[half:, :])
        res[p] = x.astype(BF16)

    each(4, results)
    factor_end(0, first)
    plane_add(4)
    column_add(2)
    factor_near(1)
    for n in range(3):
        finish(n)
    finish_last(3)
    finish_last(4)
    factor_end(1, second)


def mega_call(nz, nx, *args):
    ns = nz * nx
    rows = 4 * ns
    width = 12 * ns
    half = width // 2
    vmem, sem = pltpu.VMEM, pltpu.SemaphoreType.DMA
    scratch = [
        vmem((4, rows, width), BF16),
        vmem((4, rows, rows), BF16),
        vmem((4, rows, rows), BF16),
        vmem((width, width), BF16),
        vmem((width, width), BF16),
        vmem((width, width), BF16),
        vmem((4, rows, width), BF16),
        vmem((width, 4 * rows), BF16),
        vmem((4, rows, rows), BF16),
        vmem((4, rows, rows), BF16),
    ]
    for sizes in ((1, 2, 3), (1, 2, 3), (3, 2, 1), (3, 2, 1)):
        scratch += [vmem((ns, 16, half // 3 * size), BF16) for size in sizes]
    scratch += [
        vmem((2, 4, rows, half), BF16),
        vmem((2, 4, rows, half), F32),
        vmem((2, 4, rows, half), F32),
        vmem((2, 4, rows, half), BF16),
        vmem((4, rows, half), F32),
        vmem((4, rows, half), BF16),
        vmem((2, 4, rows, half), BF16),
        vmem((2, 4, rows, half), BF16),
        vmem((2, 4, rows, half), BF16),
        vmem((half, 4 * rows), BF16),
        vmem((3, 4 * rows, half // 3), F32),
        vmem((2, width + 8, half), F32),
    ]
    for n in range(5):
        count, _ = zone_of(nz, n)
        scratch += [
            vmem((2, nx, count, 16, half), BF16),
            vmem((nx, count, 16, half), BF16),
            vmem((nx, count, 16, half), BF16),
            vmem((nx, count, 16, half), BF16),
            vmem((count, 16, half), BF16),
            vmem((4 * nz if n > 2 else 2 * nz, 16, half), BF16),
            vmem((2, 16, half), BF16),
        ]
    scratch += [vmem((int(nx**0.5), nz, 16, half), BF16)] * 2
    for _ in range(2):
        scratch += [
            vmem((2, 2, rows, rows), BF16),
            vmem((2, rows, rows), BF16),
            vmem((2, rows, rows), BF16),
            vmem((2, rows, rows), BF16),
            vmem((2, 2, rows, rows), BF16),
        ]
    scratch += [sem((count,)) for count in (12, 6, 6, 25, 25, 12, 12)]
    anywhere = pl.BlockSpec(memory_space=pl.ANY)
    return pl.pallas_call(
        functools.partial(mega, nz, nx),
        out_shape=(vmem((4, rows, width), BF16),) * 2
        + (vmem((4, rows, rows), F32),) * 2
        + (vmem((12, width), F32),) * 3,
        in_specs=[anywhere] * 7,
        out_specs=(pl.BlockSpec(memory_space=vmem),) * 7,
        scratch_shapes=scratch,
        compiler_params=pltpu.CompilerParams(
            collective_id=0, has_side_effects=True, vmem_limit_bytes=53 * 2**20
        ),
        cost_estimate=pl.CostEstimate(
            flops=14 * 10**9, bytes_accessed=16 * 10**6, transcendentals=10**6
        ),
        name="mixing",
    )(*args)


def deliver(*refs):
    sources, targets, sem = refs[:7], refs[7:14], refs[14]
    copies = []
    for src, dst in zip(sources, targets):
        for i in range(src.shape[0] if len(src.shape) == 3 else 1):
            pair = (src.at[i], dst.at[i]) if len(src.shape) == 3 else (src, dst)
            copies.append(pltpu.make_async_copy(*pair, sem.at[len(copies)]))
    for copy in copies:
        copy.start()
    for copy in copies:
        copy.wait()


def deliver_call(arrays):
    return pl.pallas_call(
        deliver,
        out_shape=tuple(jax.ShapeDtypeStruct(x.shape, x.dtype) for x in arrays),
        in_specs=[pl.BlockSpec(memory_space=pltpu.VMEM)] * 7,
        out_specs=(pl.BlockSpec(memory_space=pl.ANY),) * 7,
        scratch_shapes=[pltpu.SemaphoreType.DMA((19,))],
        compiler_params=pltpu.CompilerParams(vmem_limit_bytes=2**20),
        name="deliver",
    )(*arrays)


def shards(
    nz, nx, tokens, first_factor, second_factor, value_weight, gate_weight, out_weight, cotangent
):
    rows, width = 4 * nz * nx, 12 * nz * nx
    arrays = mega_call(
        nz,
        nx,
        tokens.reshape(4, rows, width),
        first_factor,
        second_factor,
        value_weight,
        gate_weight,
        out_weight,
        cotangent.reshape(4, rows, width),
    )
    result, grad, first, second, value_sum, gate_sum, out_sum = deliver_call(arrays)
    return (
        result.reshape(1, 4 * rows, width),
        grad.reshape(1, 4 * rows, width),
        first,
        second,
        value_sum,
        gate_sum,
        out_sum,
    )


def solution(mesh, nz=NZ, nx=NX):
    return jax.shard_map(
        functools.partial(shards, nz, nx),
        mesh=mesh,
        in_specs=(
            P("dp", "seq", None),
            P("seq", None, None),
            P("seq", None, None),
            P(),
            P(),
            P(),
            P("dp", "seq", None),
        ),
        out_specs=(
            P("dp", "seq", None),
            P("dp", "seq", None),
            P("seq", None, None),
            P("seq", None, None),
            P("seq", None),
            P("seq", None),
            P("seq", None),
        ),
        check_vma=False,
    )
```
